128 devices in a mesh: row: 8 (over x, core), col: 16 (over z, y).
Axes of the slice: x: 4, y: 4, z: 4, core: 2. Of those that a mesh axis runs over, the one named last changes fastest.
Arguments:
- markov: bfloat16 [2, 512, 128, 128], P(None, 'col'), may hold values from -6 to 6
- omega: bfloat16 [65536, 64], P('col'), may hold values from -0.0234375 to 0.0234375
Outputs:
- denoised: float32 [2, 512, 128, 128], P(None, 'col')
The draws below stay inside these ranges and needn't reach their ends.
All inputs are finite; a program needn't handle non-finite values.
Results may differ from the reference program's by a relative error of at most 0.0007.
Values may be sent and summed in bfloat16 or wider, within the bound.
A program may use at most 64 MiB of HBM per device.

```python
import jax
import jax.numpy as jnp
from jax import lax

P_SIZE = 128
M = 128
K = 64
NS_STEPS = 8
NBR = 256
NBC = 512
COLS = 65536


def draw_markov(key, part):
    keys = jax.random.split(key, 5)
    modes = K // 2
    lag_pos = jnp.arange(2 * NBC, dtype=jnp.float32)
    radius = jnp.exp(-jax.random.uniform(keys[0], (modes,), jnp.float32, 0.0, 2.5) / (2 * NBC))
    freqs = jax.random.uniform(keys[1], (modes,), jnp.float32, 0.05, 3.0)
    left = jax.random.normal(keys[2], (2, P_SIZE, modes), jnp.float32) / jnp.sqrt(1.0 * modes)
    right = jax.random.normal(keys[3], (2, modes, M), jnp.float32)
    envelope = radius[None, :] ** lag_pos[:, None]
    cosine = envelope * jnp.cos(freqs[None, :] * lag_pos[:, None])
    sine = envelope * jnp.sin(freqs[None, :] * lag_pos[:, None])
    signal = jnp.einsum('pr,lr,rm->lpm', left[0], cosine, right[0]) + jnp.einsum('pr,lr,rm->lpm', left[1], sine, right[1])
    noise = 0.3 * jax.random.normal(keys[4], (2 * NBC, P_SIZE, M), jnp.float32)
    return jnp.clip(signal + noise, -6.0, 6.0).reshape(2, NBC, P_SIZE, M).astype(jnp.bfloat16)


def levels(stream_key, dims, cuts, least, top_value):
    gain = 1.0
    for position, blocks in cuts:
        steps = jax.random.uniform(jax.random.fold_in(jax.random.fold_in(stream_key, 6), position), (blocks,), jnp.float32, least / len(cuts), top_value / len(cuts))
        gain = gain * jnp.repeat(jnp.exp(steps), dims[position] // blocks).reshape((-1,) + (1,) * (len(dims) - 1 - position))
    return gain


def gaussian(rng, shape, spread, limit, pieces=(), kind=jnp.bfloat16):
    array = jax.random.normal(rng, shape, jnp.float32) * spread
    if len(pieces) > 0:
        array = levels(rng, shape, pieces, -0.22, 0.18) * array
    return jnp.clip(array, min=-limit, max=limit).astype(kind)


def setup_inputs(seed: int = 0) -> dict:
    streams_of = jax.random.split(jax.random.key(seed), 3)
    return {
        "markov": draw_markov(jax.random.fold_in(streams_of[2], 71), 0),
        "omega": gaussian(streams_of[1], (COLS, K), COLS ** -0.5, 0.0234375, ((0, 16),)),
    }


norm_floor = 1e-06

def reference(markov, omega):
    lag_blocks = markov.reshape(2 * NBC, P_SIZE, M).astype(jnp.float32)
    omega_blocks = omega.reshape(NBC, M, K).astype(jnp.float32)
    column_ids = jnp.arange(NBC, dtype=jnp.int32)

    def range_step(running, column_id):
        window = lax.dynamic_slice_in_dim(lag_blocks, column_id, NBR, 0)
        weights = lax.dynamic_index_in_dim(omega_blocks, column_id, 0, keepdims=False)
        return (running + jnp.einsum('ipm,mk->ipk', window, weights), None)
    sketch, _ = lax.scan(range_step, jnp.zeros((NBR, P_SIZE, K), jnp.float32), column_ids)
    sketch = sketch.reshape(NBR * P_SIZE, K)
    gram = jnp.dot(sketch.T, sketch, precision=lax.Precision.HIGHEST, preferred_element_type=jnp.float32)
    current = sketch / jnp.sqrt(jnp.trace(gram) + norm_floor)
    for sweep in range(NS_STEPS):
        inner = jnp.dot(current.T, current, precision=lax.Precision.HIGHEST, preferred_element_type=jnp.float32)
        current = 1.5 * current - 0.5 * jnp.dot(current, inner, precision=lax.Precision.HIGHEST, preferred_element_type=jnp.float32)
    basis = current.astype(jnp.bfloat16)
    basis_f = basis.astype(jnp.float32).reshape(NBR, P_SIZE, K)

    def projection_update(carry, column_id):
        window = lax.dynamic_slice_in_dim(lag_blocks, column_id, NBR, 0)
        return (carry, jnp.einsum('ipk,ipm->km', basis_f, window))
    _, projected_matrix = lax.scan(projection_update, 0.0, column_ids)
    projected_matrix = projected_matrix.astype(jnp.bfloat16)
    projected_matrix = lax.optimization_barrier(projected_matrix).astype(jnp.float32)

    def lag_step(running, inputs):
        row_position, orthonormal_row_vector = inputs
        summand_terms = jnp.einsum('fb,gby->gfy', orthonormal_row_vector, projected_matrix)
        current_sum = lax.dynamic_slice_in_dim(running, row_position, NBC, 0)
        return (lax.dynamic_update_slice_in_dim(running, current_sum + summand_terms, row_position, 0), None)
    totals, _ = lax.scan(lag_step, jnp.zeros((NBR + NBC, P_SIZE, M), jnp.float32), (jnp.arange(NBR, dtype=jnp.int32), basis_f))
    totals = jnp.pad(totals, ((0, 2 * NBC - NBR - NBC), (0, 0), (0, 0)))
    lag_ids = jnp.arange(2 * NBC, dtype=jnp.int32)
    counts = jnp.maximum(jnp.minimum(lag_ids, NBR - 1) - jnp.maximum(0, lag_ids - NBC + 1) + 1, 0)
    counts_f = counts.astype(jnp.float32)[:, None, None]
    averaged = totals / jnp.maximum(counts_f, 1.0)
    merged = jnp.where(counts_f > 0, 0.5 * lag_blocks + 0.5 * averaged, lag_blocks)
    return merged.reshape(2, NBC, P_SIZE, M)
```

```python
import functools

import jax
import jax.numpy as jnp
from jax import lax
from jax.experimental import pallas as pl
from jax.experimental.pallas import tpu as pltpu
from jax.sharding import PartitionSpec as P

NS_STEPS = 8
norm_floor = 1e-06
highest = lax.Precision.HIGHEST
MESH = pl.DeviceIdType.MESH
KH = 32
B = 128
f32, bf16 = jnp.float32, jnp.bfloat16
NT_DIMS = (((1,), (1,)), ((), ()))


def mm(left, right, **kw):
    return jnp.dot(left, right, preferred_element_type=f32, **kw)


def mm_nt(left, right, **kw):
    return lax.dot_general(left, right, NT_DIMS, preferred_element_type=f32, **kw)


def kernel(
    X, C, nb, SDT,
    l_ref, om_ref, out_ref,
    wl, q, omp, acc, s_send, s_recv, s_full, g_own, gx_recv, g_x, gc_recv, p_ref,
    bp, bpt, pacc, pr_send, pr_recv, prb, prx, tot, tx_send, tx_recv, ch, xr,
    l_sem, om_s, om_r, s_s, s_r, sx_s, sx_r, gx_s, gx_r, gc_s, gc_r, b_s, b_r,
    pr_s, pr_r, pa_s, pa_r, tx_s, tx_r, xr_s, xr_r, ag_s, ag_r, fx_s, fx_r,
):
    NT = nb // 2
    PO = nb // C
    PQ = NT // X
    LQ = NT // X
    r = lax.axis_index("row")
    c = lax.axis_index("col")
    x, core = r // 2, r % 2

    def dev(xx, cc, kk=None):
        return (xx * 2 + (core if kk is None else kk), cc)

    def col(dc):
        return lax.rem(c + dc + 4 * C, C)

    def xat(dx):
        return lax.rem(x + dx, X)

    def xcol(dx, delta):
        xx = xat(dx)
        return dev(xx, lax.rem(c + 2 * (xx - x) + delta + 4 * C, C))

    def remote(src, dst, send, recv, device):
        return pltpu.make_async_remote_copy(
            src_ref=src, dst_ref=dst, send_sem=send, recv_sem=recv, device_id=device, device_id_type=MESH
        )

    halves = [jnp.where(c - 2 * x - e < 0, 1, 0).astype(jnp.int32) for e in range(3)]

    loads = []
    for h in range(2):
        for s in range(2):
            loads.append(
                pltpu.make_async_copy(
                    l_ref.at[h],
                    wl.at[h, pl.ds((1 + s) * B, nb * B), pl.ds(s * B, B)],
                    l_sem.at[2 * h + s],
                )
            )
    for cp in loads:
        cp.start()

    barrier = pltpu.get_barrier_semaphore()
    peers = [dev(x, col(dc)) for dc in range(1, C)]
    for dx in range(1, X):
        peers += [xcol(dx, delta) for delta in (-1, 0, 1)] + [dev(xat(dx), c)]
    peers.append(dev(x, c, 1 - core))
    for peer in peers:
        pl.semaphore_signal(barrier, inc=1, device_id=peer, device_id_type=MESH)

    pick = jnp.where(
        lax.broadcasted_iota(jnp.int32, (KH, 2 * KH), 1)
        == lax.broadcasted_iota(jnp.int32, (KH, 2 * KH), 0) + core * KH,
        1.0, 0.0,
    ).astype(bf16)
    for w in range(NT):
        both = mm_nt(pick, om_ref[w * 2 * B : (w + 1) * 2 * B, :]).astype(bf16)
        n = NT - 1 - w
        q[n * KH : (n + 1) * KH, :B] = both[:, B:]
        q[n * KH : (n + 1) * KH, B:] = both[:, :B]

    pl.semaphore_wait(barrier, len(peers))

    pending = []

    om_self = [lax.rem(2 * x + e, C) == 0 for e in range(3)]
    om_copies = []
    for e in range(3):
        cp = remote(q, omp.at[e], om_s.at[e], om_r.at[e], dev(x, col(2 * x + e)))
        om_copies.append(cp)

        @pl.when(jnp.logical_not(om_self[e]))
        def _():
            cp.start()

        @pl.when(om_self[e])
        def _():
            omp[e] = q[...]

    for h in range(2):
        zero = jnp.zeros((B, B), bf16)
        wl[h, 0:B, 0:B] = zero
        wl[h, 0:B, B:] = zero
        wl[h, B : 2 * B, B:] = zero
        wl[h, (nb + 1) * B :, 0:B] = zero
    bp[0 : NT * KH, :] = jnp.zeros((NT * KH, 2 * B), bf16)
    bp[3 * NT * KH :, :] = jnp.zeros((NT * KH, 2 * B), bf16)
    acc[...] = jnp.zeros_like(acc)
    for cp in loads:
        cp.wait()

    HB = NT // 2
    blocks = {
        0: ((0, HB, HB + 1, NT + 1), (HB, HB, 1, NT + 1)),
        1: ((0, NT, 0, NT + 1),),
        2: ((0, HB, 0, NT), (HB, HB, 0, HB)),
    }

    for e in range(3):
        @pl.when(jnp.logical_not(om_self[e]))
        def _():
            om_copies[e].wait_recv()

        for start, size, lo, hi in blocks[e]:
            rows = size * KH

            def step(tau, carry):
                left = omp[e, start * KH : start * KH + rows, :]
                right = wl[halves[e], pl.ds(pl.multiple_of(tau * 2 * B, 2 * B), 2 * B), :]
                at = pl.ds(pl.multiple_of((e * NT + start + tau) * KH, KH), rows)
                acc[at, :] += mm_nt(left, right)
                return carry

            lax.fori_loop(lo, hi, step, 0)

    s_send[...] = acc[NT * KH : 3 * NT * KH, :].astype(SDT)
    srows = PO * KH
    copies = []
    for dc in range(1, C):
        dst = col(dc)
        cp = remote(
            s_send.at[pl.ds(pl.multiple_of(dst * srows, srows), srows)], s_recv.at[dc],
            s_s.at[dc], s_r.at[dc], dev(x, dst),
        )
        cp.start()
        copies.append(cp)
    total = acc[pl.ds(pl.multiple_of((NT + c * PO) * KH, KH), srows), :]
    for dc in range(1, C):
        copies[dc - 1].wait_recv()
        total = total + s_recv[dc].astype(f32)
    pending += copies
    s_full[core] = total
    cp = remote(s_full.at[core], s_full.at[core], sx_s, sx_r, dev(x, c, 1 - core))
    cp.start()
    cp.wait_recv()
    pending.append(cp)

    sk = jnp.concatenate(
        [
            jnp.concatenate([s_full[k, o * KH : (o + 1) * KH, :] for k in range(2)], axis=0)
            for o in range(PO)
        ],
        axis=1,
    )
    gram = mm_nt(sk, sk, precision=highest)
    g_own[...] = jnp.concatenate([gram[:KH], gram[KH:]], axis=1)
    copies = []
    for dx in range(1, X):
        cp = remote(g_own, gx_recv.at[dx], gx_s.at[dx], gx_r.at[dx], dev(xat(dx), c))
        cp.start()
        copies.append(cp)
    packed = g_own[...]
    for dx in range(1, X):
        copies[dx - 1].wait_recv()
        packed = packed + gx_recv[dx]
    pending += copies
    g_x[...] = packed
    copies = []
    for dc in range(1, C):
        cp = remote(g_x, gc_recv.at[dc], gc_s.at[dc], gc_r.at[dc], dev(x, col(dc)))
        cp.start()
        copies.append(cp)
    for dc in range(1, C):
        copies[dc - 1].wait_recv()
        packed = packed + gc_recv[dc]
    pending += copies
    gram = jnp.concatenate([packed[:, : 2 * KH], packed[:, 2 * KH :]], axis=0)

    eye = (
        lax.broadcasted_iota(jnp.int32, (2 * KH, 2 * KH), 0)
        == lax.broadcasted_iota(jnp.int32, (2 * KH, 2 * KH), 1)
    ).astype(f32)
    trace = jnp.sum(gram * eye)
    scale = 1.0 / jnp.sqrt(jnp.full((1, 1), trace, f32) + norm_floor)
    inner = gram * (scale * scale)
    prod = None
    for sweep in range(NS_STEPS):
        a = 1.5 * eye - 0.5 * inner
        prod = a if prod is None else mm(prod, a, precision=highest)
        if sweep < NS_STEPS - 1:
            inner = mm(a, mm(inner, a, precision=highest), precision=highest)
    p_ref[...] = prod * scale

    basis = mm(p_ref[pl.ds(pl.multiple_of(core * KH, KH), KH), :], sk, precision=highest).astype(bf16)
    mine = pl.multiple_of((NT + c * PO) * KH, KH)
    for o in range(PO):
        bp[pl.ds(pl.multiple_of(mine + o * KH, KH), KH), :] = basis[:, o * 2 * B : (o + 1) * 2 * B]
    copies = []
    for dc in range(1, C):
        at = bp.at[pl.ds(mine, srows)]
        cp = remote(at, at, b_s.at[dc], b_r.at[dc], dev(x, col(dc)))
        cp.start()
        copies.append(cp)
    for cp in copies:
        cp.wait_recv()
    pending += copies

    qrows = PQ * KH
    pr_copies = {}
    for e in (0, 2, 1):
        pacc[...] = jnp.zeros_like(pacc)
        for start, size, lo, hi in blocks[e]:
            rows = size * KH

            def step(tau, carry):
                at = pl.ds(pl.multiple_of((e * NT + start + tau) * KH, KH), rows)
                right = wl[halves[e], pl.ds(pl.multiple_of(tau * 2 * B, 2 * B), 2 * B), :]
                pacc[start * KH : start * KH + rows, :] += mm(bp[at, :], right)
                return carry

            lax.fori_loop(lo, hi, step, 0)
        pr_send[e] = pacc[...].astype(bf16)
        for dx in range(X):
            if dx == 0 and e == 1:
                continue
            slot = dx * 3 + e
            cp = remote(
                pr_send.at[e, pl.ds(pl.multiple_of(xat(dx) * qrows, qrows), qrows)], pr_recv.at[slot],
                pr_s.at[slot], pr_r.at[slot], xcol(dx, 1 - e),
            )
            cp.start()
            pr_copies[slot] = cp

    for g in range(NT):
        first = (NT + 2 * g) * KH
        pieces = [
            bp[first + o * KH : first + (o + 1) * KH, s * B : (s + 1) * B] for o in range(2) for s in range(2)
        ]
        bpt[:, g * B : (g + 1) * B] = jnp.concatenate(pieces, axis=0).T

    quarter = pl.ds(pl.multiple_of(x * qrows, qrows), qrows)
    total = pacc[quarter, :]
    for slot, cp in pr_copies.items():
        cp.wait_recv()
        total = total + pr_recv[slot].astype(f32)
    pending += list(pr_copies.values())
    prb[1, quarter, :] = total.astype(bf16)
    copies = []
    for dx in range(X):
        for e in range(3):
            if dx == 0 and e == 1:
                continue
            slot = dx * 3 + e
            cp = remote(
                prb.at[1, quarter], prb.at[e, quarter], pa_s.at[slot], pa_r.at[slot], xcol(dx, e - 1)
            )
            cp.start()
            copies.append(cp)
    for cp in copies:
        cp.wait_recv()
    pending += copies

    def active(h, xx):
        return c - 2 * xx >= 0 if h == 0 else c - 2 * xx - 2 < 0

    tx_copies = []
    for h in range(2):
        cp = remote(tx_send.at[h], tx_recv.at[h], tx_s.at[h], tx_r.at[h], dev(x, c, 1 - core))
        tx_copies.append(cp)

        @pl.when(active(h, x))
        def _():
            for e in range(3):
                @pl.when(halves[e] == h)
                def _():
                    for i in range(NT):
                        n = e * NT + i
                        pair = prb[e, i * KH : (i + 1) * KH, :]
                        prx[n, 0:KH, :] = pair
                        prx[n, KH:, :B] = pair[:, B:]
                        if n > 0:
                            prx[n - 1, KH:, B:] = pair[:, :B]

                @pl.when(halves[e] != h)
                def _():
                    for i in range(NT):
                        n = e * NT + i
                        prx[n, 0:KH, :] = jnp.zeros((KH, 2 * B), bf16)
                        prx[n, KH:, :B] = jnp.zeros((KH, B), bf16)
                        if n > 0:
                            prx[n - 1, KH:, B:] = jnp.zeros((KH, B), bf16)

            def lag_pair(tp):
                right = prx[pl.ds(NT - 1 - tp, 2 * NT)].reshape(4 * NT * KH, 2 * B)
                return mm(bpt[...], right)

            def other(i, carry):
                value = lag_pair((1 - core) * HB + i).astype(bf16)
                tx_send[h, 2 * i] = value[:, B:]
                tx_send[h, 2 * i + 1] = value[:, :B]
                return carry

            lax.fori_loop(0, HB, other, 0)
            cp.start()

            def this(i, carry):
                value = lag_pair(core * HB + i)
                tot[h, 2 * i] = value[:, B:]
                tot[h, 2 * i + 1] = value[:, :B]
                return carry

            lax.fori_loop(0, HB, this, 0)

    nbr, nbc = 2 * nb * X, nb * C

    def lag_of(h, t):
        return h * nbc + c * nb + core * NT + t

    def pairs_of(lag, first, last):
        low = jnp.maximum(first, lag - (nbc - 1))
        return jnp.maximum(jnp.minimum(last, lag) - low + 1, 0).astype(f32)

    def measured(h, t):
        return wl[h, pl.ds(pl.multiple_of((core * NT + t + 1) * B, B), B), 0:B].astype(f32)

    xr_sends = []
    for h in range(2):
        sends = []
        for dx in range(1, X):
            xx = xat(dx)
            sends.append(
                remote(
                    ch.at[h, pl.ds(xx * LQ, LQ)], xr.at[h, dx], xr_s.at[h * X + dx], xr_r.at[h * X + dx],
                    dev(xx, c),
                )
            )
        xr_sends.append(sends)

        @pl.when(active(h, x))
        def _():
            tx_copies[h].wait_recv()

            def combine(t, carry):
                n = pairs_of(lag_of(h, t), 2 * nb * x, 2 * nb * (x + 1) - 1)
                value = tot[h, t] + tx_recv[h, t].astype(f32) - (0.5 * n) * measured(h, t)
                tot[h, t] = value
                ch[h, t] = value.astype(bf16)
                return carry

            lax.fori_loop(0, NT, combine, 0)
            for cp in sends:
                cp.start()

    ag_copies, fx_copies = [], []
    has = [None, c < 2 * X]
    for h in range(2):
        def finish():
            at0 = core * NT + x * LQ

            @pl.when(jnp.logical_not(active(h, x)))
            def _():
                for i in range(LQ):
                    tot[h, x * LQ + i] = jnp.zeros((B, B), f32)

            for dx in range(1, X):
                src = lax.rem(x - dx + X, X)

                @pl.when(active(h, src))
                def _():
                    xr_sends[h][dx - 1].wait_recv()
                    for i in range(LQ):
                        tot[h, x * LQ + i] += xr[h, dx, i].astype(f32)

            for i in range(LQ):
                n = pairs_of(lag_of(h, x * LQ + i), 0, nbr - 1)
                value = tot[h, x * LQ + i] / jnp.maximum(n, 1.0)
                out_ref[h, at0 + i] = value.astype(bf16)

        at = out_ref.at[h, pl.ds(core * NT + x * LQ, LQ)]
        sends = [
            remote(at, at, ag_s.at[h * X + dx], ag_r.at[h * X + dx], dev(xat(dx), c)) for dx in range(1, X)
        ]
        mine_at = out_ref.at[h, pl.ds(core * NT, NT)]
        across = remote(mine_at, mine_at, fx_s.at[h], fx_r.at[h], dev(x, c, 1 - core))
        ag_copies.append(sends)
        fx_copies.append(across)

        def spread():
            finish()
            for cp in sends:
                cp.start()

        if h == 0:
            spread()
        else:
            pl.when(has[1])(spread)

            @pl.when(jnp.logical_not(has[1]))
            def _():
                out_ref[1] = jnp.zeros((nb, B, B), bf16)

    def gather(h):
        for cp in ag_copies[h]:
            cp.wait_recv()
        fx_copies[h].start()

    gather(0)
    pl.when(has[1])(functools.partial(gather, 1))

    def settle(h):
        fx_copies[h].wait_recv()
        for cp in ag_copies[h]:
            cp.wait_send()
        fx_copies[h].wait_send()

    settle(0)
    pl.when(has[1])(functools.partial(settle, 1))
    for h in range(2):
        @pl.when(active(h, x))
        def _():
            tx_copies[h].wait_send()
            for cp in xr_sends[h]:
                cp.wait_send()

    for e in range(3):
        @pl.when(jnp.logical_not(om_self[e]))
        def _():
            om_copies[e].wait_send()

    for cp in pending:
        cp.wait_send()


def local(X, C, SDT, markov, omega):
    halves, nb = markov.shape[:2]
    NT = nb // 2
    PO, PQ, LQ = nb // C, NT // X, NT // X
    vmem, dma = pltpu.VMEM, pltpu.SemaphoreType.DMA
    scratch = [
        vmem((2, (nb + 2) * B, 2 * B), bf16),
        vmem((NT * KH, 2 * B), bf16),
        vmem((3, NT * KH, 2 * B), bf16),
        vmem(((4 * NT + 1) * KH, 2 * B), f32),
        vmem((2 * NT * KH, 2 * B), SDT),
        vmem((C, PO * KH, 2 * B), SDT),
        vmem((2, PO * KH, 2 * B), f32),
        vmem((KH, 4 * KH), f32),
        vmem((X, KH, 4 * KH), f32),
        vmem((KH, 4 * KH), f32),
        vmem((C, KH, 4 * KH), f32),
        vmem((2 * KH, 2 * KH), f32),
        vmem((4 * NT * KH, 2 * B), bf16),
        vmem((B, NT * B), bf16),
        vmem((NT * KH, 2 * B), f32),
        vmem((3, NT * KH, 2 * B), bf16),
        vmem((3 * X, PQ * KH, 2 * B), bf16),
        vmem((3, NT * KH, 2 * B), bf16),
        vmem((3 * NT, 2 * KH, 2 * B), bf16),
        vmem((2, NT, B, B), f32),
        vmem((2, NT, B, B), bf16),
        vmem((2, NT, B, B), bf16),
        vmem((2, NT, B, B), bf16),
        vmem((2, X, LQ, B, B), bf16),
        dma((4,)),
        dma((3,)), dma((3,)), dma((C,)), dma((C,)), dma, dma,
        dma((X,)), dma((X,)), dma((C,)), dma((C,)), dma((C,)), dma((C,)),
        dma((3 * X,)), dma((3 * X,)), dma((3 * X,)), dma((3 * X,)),
        dma((2,)), dma((2,)), dma((2 * X,)), dma((2 * X,)), dma((2 * X,)), dma((2 * X,)),
        dma((2,)), dma((2,)),
    ]
    excess = pl.pallas_call(
        functools.partial(kernel, X, C, nb, SDT),
        out_shape=jax.ShapeDtypeStruct((halves, nb, B, B), bf16),
        in_specs=[pl.BlockSpec(memory_space=pl.ANY), pl.BlockSpec(memory_space=pltpu.VMEM)],
        out_specs=pl.BlockSpec(memory_space=pltpu.VMEM),
        scratch_shapes=scratch,
        compiler_params=pltpu.CompilerParams(
            collective_id=0, has_side_effects=True, vmem_limit_bytes=48 * 2**20
        ),
        name="cadzow",
    )(markov.reshape(halves, nb * B, B), omega)
    lags = (
        jnp.arange(2, dtype=jnp.int32)[:, None] * (nb * C)
        + lax.axis_index("col") * nb
        + jnp.arange(nb, dtype=jnp.int32)[None, :]
    )
    counts = jnp.minimum(lags, 2 * nb * X - 1) - jnp.maximum(0, lags - nb * C + 1) + 1
    measured = markov.astype(f32)
    merged = 0.75 * measured + 0.5 * excess.astype(f32)
    return jnp.where((counts > 0)[:, :, None, None], merged, measured)


def solution(mesh):
    X, C = mesh.shape["row"] // 2, mesh.shape["col"]
    in_specs = (P(None, "col", None, None), P("col", None))
    return jax.shard_map(
        functools.partial(local, X, C, bf16),
        mesh=mesh,
        in_specs=in_specs,
        out_specs=P(None, "col", None, None),
        check_vma=False,
    )
```

```python
import functools

import jax
import jax.numpy as jnp
from jax import lax
from jax.experimental import pallas as pl
from jax.experimental.pallas import tpu as pltpu
from jax.sharding import PartitionSpec as P

NS_STEPS = 8
norm_floor = 1e-06
highest = lax.Precision.HIGHEST
MESH = pl.DeviceIdType.MESH
KH = 32
B = 128
f32, bf16 = jnp.float32, jnp.bfloat16
NT_DIMS = (((1,), (1,)), ((), ()))


def mm(left, right, **kw):
    return jnp.dot(left, right, preferred_element_type=f32, **kw)


def mm_nt(left, right, **kw):
    return lax.dot_general(left, right, NT_DIMS, preferred_element_type=f32, **kw)


def kernel(
    X, C, nb, SDT,
    l_ref, om_ref, out_ref,
    wl, q, omp, acc, s_send, s_recv, s_full, g_own, gx_recv, g_x, gc_recv, p_ref,
    bp, bpt, pacc, pr_send, pr_recv, prb, prx, tot, tx_send, tx_recv, ch, xr,
    l_sem, om_s, om_r, s_s, s_r, sx_s, sx_r, gx_s, gx_r, gc_s, gc_r, b_s, b_r,
    pr_s, pr_r, pa_s, pa_r, tx_s, tx_r, xr_s, xr_r, ag_s, ag_r, fx_s, fx_r,
):
    NT = nb // 2
    HB = NT // 2
    PO = nb // C
    PQ = NT // X
    LQ = NT // X
    r = lax.axis_index("row")
    c = lax.axis_index("col")
    x, core = r // 2, r % 2

    def dev(xx, cc, kk=None):
        return (xx * 2 + (core if kk is None else kk), cc)

    def col(dc):
        return lax.rem(c + dc + 4 * C, C)

    def xat(dx):
        return lax.rem(x + dx, X)

    def xcol(dx, delta):
        xx = xat(dx)
        return dev(xx, lax.rem(c + 2 * (xx - x) + delta + 4 * C, C))

    def remote(src, dst, send, recv, device):
        return pltpu.make_async_remote_copy(
            src_ref=src, dst_ref=dst, send_sem=send, recv_sem=recv, device_id=device, device_id_type=MESH
        )

    halves = [jnp.where(c - 2 * x - e < 0, 1, 0).astype(jnp.int32) for e in range(3)]

    barrier = pltpu.get_barrier_semaphore()
    peers = [dev(x, col(dc)) for dc in range(1, C)]
    for dx in range(1, X):
        peers += [xcol(dx, delta) for delta in (-1, 0, 1)] + [dev(xat(dx), c)]
    peers.append(dev(x, c, 1 - core))
    for peer in peers:
        pl.semaphore_signal(barrier, inc=1, device_id=peer, device_id_type=MESH)

    loads = []
    for h in range(2):
        for s in range(2):
            loads.append(
                pltpu.make_async_copy(
                    l_ref.at[h],
                    wl.at[h, pl.ds((1 + s) * B, nb * B), pl.ds(s * B, B)],
                    l_sem.at[2 * h + s],
                )
            )
    for cp in loads:
        cp.start()
    half_rank = pl.ds(pl.multiple_of(core * KH, KH), KH)
    for w in range(NT):
        n = NT - 1 - w
        q[n * KH : (n + 1) * KH, :B] = om_ref[half_rank, (2 * w + 1) * B : (2 * w + 2) * B]
        q[n * KH : (n + 1) * KH, B:] = om_ref[half_rank, 2 * w * B : (2 * w + 1) * B]
    zero = jnp.zeros((B, B), bf16)
    for h in range(2):
        wl[h, 0:B, 0:B] = zero
        wl[h, 0:B, B:] = zero
        wl[h, B : 2 * B, B:] = zero
        wl[h, (nb + 1) * B :, 0:B] = zero
    bp[0 : NT * KH, :] = jnp.zeros((NT * KH, 2 * B), bf16)
    bp[3 * NT * KH :, :] = jnp.zeros((NT * KH, 2 * B), bf16)
    PAD = PQ - 1
    for e in range(3):
        omp[e, 0 : PAD * KH, :] = jnp.zeros((PAD * KH, 2 * B), bf16)
        omp[e, (PAD + NT) * KH :, :] = jnp.zeros((PAD * KH, 2 * B), bf16)
    pl.semaphore_wait(barrier, len(peers))

    pending = []

    om_self = [lax.rem(2 * x + e, C) == 0 for e in range(3)]
    om_copies = []
    for e in range(3):
        cp = remote(q, omp.at[e, pl.ds(PAD * KH, NT * KH)], om_s.at[e], om_r.at[e], dev(x, col(2 * x + e)))
        om_copies.append(cp)

        @pl.when(jnp.logical_not(om_self[e]))
        def _():
            cp.start()

        @pl.when(om_self[e])
        def _():
            omp[e, PAD * KH : (PAD + NT) * KH, :] = q[...]

    for cp in loads:
        cp.wait()

    def lags(e, tau):
        return wl[halves[e], tau * 2 * B : (tau + 1) * 2 * B, :]

    srows, brows = PO * KH, PQ * KH
    s_copies = []

    def send_sketch(first, last):
        for dst in range(first, last):
            dc = lax.rem(dst - c + C, C)
            cp = remote(
                s_send.at[pl.ds(dst * srows, srows)], s_recv.at[dc], s_s.at[dc], s_r.at[dc], dev(x, dst)
            )
            pl.when(dst != c)(cp.start)

    started = set()
    for e in range(3):
        @pl.when(jnp.logical_not(om_self[e]))
        def _():
            om_copies[e].wait_recv()

        for b in range(0, 2 * NT, PQ):
            value = None
            for tau in range(NT + 1):
                n = b + NT - tau - e * NT
                if -PQ < n < NT:
                    left = omp[e, (PAD + n) * KH : (PAD + n) * KH + brows, :]
                    term = mm_nt(left, lags(e, tau))
                    value = term if value is None else value + term
            if value is None:
                continue
            rows = slice(b * KH, b * KH + brows)
            if b in started:
                value = value + acc[rows, :]
            started.add(b)
            acc[rows, :] = value
            if (e == 1 and b < NT) or e == 2:
                s_send[rows, :] = value.astype(SDT)
        if e > 0:
            send_sketch((e - 1) * C // 2, e * C // 2)

    for dc in range(1, C):
        s_copies.append(
            remote(s_send.at[pl.ds(0, srows)], s_recv.at[dc], s_s.at[dc], s_r.at[dc], dev(x, col(dc)))
        )
    total = acc[pl.ds(pl.multiple_of(c * srows, srows), srows), :]
    for dc in range(1, C):
        s_copies[dc - 1].wait_recv()
        total = total + s_recv[dc].astype(f32)
    pending += s_copies
    s_full[core] = total
    cp = remote(s_full.at[core], s_full.at[core], sx_s, sx_r, dev(x, c, 1 - core))
    cp.start()
    cp.wait_recv()
    pending.append(cp)

    sk = jnp.concatenate(
        [
            jnp.concatenate([s_full[k, o * KH : (o + 1) * KH, :] for k in range(2)], axis=0)
            for o in range(PO)
        ],
        axis=1,
    )
    gram = mm_nt(sk, sk, precision=highest)
    g_own[...] = jnp.concatenate([gram[:KH], gram[KH:]], axis=1)
    copies = []
    for dx in range(1, X):
        cp = remote(g_own, gx_recv.at[dx], gx_s.at[dx], gx_r.at[dx], dev(xat(dx), c))
        cp.start()
        copies.append(cp)
    packed = g_own[...]
    for dx in range(1, X):
        copies[dx - 1].wait_recv()
        packed = packed + gx_recv[dx]
    pending += copies
    g_x[...] = packed
    copies = []
    for dc in range(1, C):
        cp = remote(g_x, gc_recv.at[dc], gc_s.at[dc], gc_r.at[dc], dev(x, col(dc)))
        cp.start()
        copies.append(cp)
    for dc in range(1, C):
        copies[dc - 1].wait_recv()
        packed = packed + gc_recv[dc]
    pending += copies
    gram = jnp.concatenate([packed[:, : 2 * KH], packed[:, 2 * KH :]], axis=0)

    eye = (
        lax.broadcasted_iota(jnp.int32, (2 * KH, 2 * KH), 0)
        == lax.broadcasted_iota(jnp.int32, (2 * KH, 2 * KH), 1)
    ).astype(f32)
    trace = jnp.sum(gram * eye)
    scale = 1.0 / jnp.sqrt(jnp.full((1, 1), trace, f32) + norm_floor)
    inner = gram * (scale * scale)
    prod = None
    for sweep in range(NS_STEPS):
        a = 1.5 * eye - 0.5 * inner
        prod = a if prod is None else mm(prod, a, precision=highest)
        if sweep < NS_STEPS - 1:
            inner = mm(a, mm(inner, a, precision=highest), precision=highest)
    p_ref[...] = prod * scale

    basis = mm(p_ref[pl.ds(pl.multiple_of(core * KH, KH), KH), :], sk, precision=highest).astype(bf16)
    mine = pl.multiple_of((NT + c * PO) * KH, KH)
    for o in range(PO):
        bp[pl.ds(pl.multiple_of(mine + o * KH, KH), KH), :] = basis[:, o * 2 * B : (o + 1) * 2 * B]
    copies = []
    for dc in range(1, C):
        at = bp.at[pl.ds(mine, srows)]
        cp = remote(at, at, b_s.at[dc], b_r.at[dc], dev(x, col(dc)))
        cp.start()
        copies.append(cp)
    for cp in copies:
        cp.wait_recv()
    pending += copies

    qrows = PQ * KH
    pr_copies = {}
    for dx in range(X):
        for e in range(3):
            if dx > 0 or e != 1:
                slot = dx * 3 + e
                pr_copies[slot] = remote(
                    pr_send.at[e, pl.ds(0, qrows)], pr_recv.at[slot], pr_s.at[slot], pr_r.at[slot],
                    xcol(dx, 1 - e),
                )
    for e in (0, 2, 1):
        for b in range(0, NT, PQ):
            value = None
            for tau in range(NT + 1):
                if (e == 0 and b + PQ - 1 < NT - tau) or (e == 2 and b >= NT - tau):
                    continue
                first = (e * NT + b + tau) * KH
                term = mm(bp[first : first + qrows, :], lags(e, tau))
                value = term if value is None else value + term
            rows = slice(b * KH, b * KH + qrows)
            pr_send[e, rows, :] = value.astype(bf16)
            if e == 1:
                pacc[rows, :] = value
            owner = b // PQ
            dx = lax.rem(owner - x + X, X)
            slot = dx * 3 + e
            cp = remote(
                pr_send.at[e, pl.ds(b * KH, qrows)], pr_recv.at[slot], pr_s.at[slot], pr_r.at[slot],
                dev(owner, lax.rem(c + 2 * (owner - x) + 1 - e + 4 * C, C)),
            )
            if e == 1:
                pl.when(owner != x)(cp.start)
            else:
                cp.start()

    for g in range(NT):
        first = (NT + 2 * g) * KH
        pieces = [
            bp[first + o * KH : first + (o + 1) * KH, s * B : (s + 1) * B] for o in range(2) for s in range(2)
        ]
        bpt[:, g * B : (g + 1) * B] = jnp.concatenate(pieces, axis=0).T

    quarter = pl.ds(pl.multiple_of(x * qrows, qrows), qrows)
    total = pacc[quarter, :]
    for slot, cp in pr_copies.items():
        cp.wait_recv()
        total = total + pr_recv[slot].astype(f32)
    pending += list(pr_copies.values())
    prb[1, quarter, :] = total.astype(bf16)
    copies = []
    for dx in range(X):
        for e in range(3):
            if dx == 0 and e == 1:
                continue
            slot = dx * 3 + e
            cp = remote(
                prb.at[1, quarter], prb.at[e, quarter], pa_s.at[slot], pa_r.at[slot], xcol(dx, e - 1)
            )
            cp.start()
            copies.append(cp)
    for cp in copies:
        cp.wait_recv()
    pending += copies

    def active(h, xx):
        return c - 2 * xx >= 0 if h == 0 else c - 2 * xx - 2 < 0

    nbr, nbc = 2 * nb * X, nb * C

    def lag_of(h, t):
        return h * nbc + c * nb + core * NT + t

    def pairs_of(lag, first, last):
        low = jnp.maximum(first, lag - (nbc - 1))
        return jnp.maximum(jnp.minimum(last, lag) - low + 1, 0).astype(f32)

    def measured(h, t):
        return wl[h, pl.ds(pl.multiple_of((core * NT + t + 1) * B, B), B), 0:B].astype(f32)

    order = sorted(range(1, X), key=lambda dx: -min(dx, X - dx)) + [0]
    tx_copies, xr_sends = [], []
    for h in range(2):
        across, sends = [], {}
        for k, dx in enumerate(order):
            across.append(
                remote(
                    tx_send.at[h, k], tx_recv.at[h, k], tx_s.at[h * X + k], tx_r.at[h * X + k],
                    dev(x, c, 1 - core),
                )
            )
            if dx > 0:
                sends[dx] = remote(
                    ch.at[h, k], xr.at[h, dx], xr_s.at[h * X + dx], xr_r.at[h * X + dx], dev(xat(dx), c)
                )
        tx_copies.append(across)
        xr_sends.append(sends)

        @pl.when(active(h, x))
        def _():
            for e in range(3):
                @pl.when(halves[e] == h)
                def _():
                    for i in range(NT):
                        n = e * NT + i
                        pair = prb[e, i * KH : (i + 1) * KH, :]
                        prx[n, 0:KH, :] = pair
                        prx[n, KH:, :B] = pair[:, B:]
                        if n > 0:
                            prx[n - 1, KH:, B:] = pair[:, :B]

                @pl.when(halves[e] != h)
                def _():
                    for i in range(NT):
                        n = e * NT + i
                        prx[n, 0:KH, :] = jnp.zeros((KH, 2 * B), bf16)
                        prx[n, KH:, :B] = jnp.zeros((KH, B), bf16)
                        if n > 0:
                            prx[n - 1, KH:, B:] = jnp.zeros((KH, B), bf16)

            def lag_pair(tp):
                right = prx[pl.ds(NT - 1 - tp, 2 * NT)].reshape(4 * NT * KH, 2 * B)
                return mm(bpt[...], right)

            def combine(k):
                dx = order[k]
                across[k].wait_recv()
                for i in range(LQ):
                    t = xat(dx) * LQ + i
                    n = pairs_of(lag_of(h, t), 2 * nb * x, 2 * nb * (x + 1) - 1)
                    value = tot[h, k, i] + tx_recv[h, k, i].astype(f32) - (0.5 * n) * measured(h, t)
                    if dx > 0:
                        ch[h, k, i] = value.astype(bf16)
                    else:
                        tot[h, k, i] = value
                if dx > 0:
                    sends[dx].start()

            for k, dx in enumerate(order):
                first = xat(dx) * (LQ // 2)
                for i in range(LQ // 2):
                    value = lag_pair((1 - core) * HB + first + i).astype(bf16)
                    tx_send[h, k, 2 * i] = value[:, B:]
                    tx_send[h, k, 2 * i + 1] = value[:, :B]
                across[k].start()
                for i in range(LQ // 2):
                    value = lag_pair(core * HB + first + i)
                    tot[h, k, 2 * i] = value[:, B:]
                    tot[h, k, 2 * i + 1] = value[:, :B]
                if k > 0:
                    combine(k - 1)
            combine(X - 1)

    has = [None, c < 2 * X]
    ag_copies, fx_copies = [], []

    def piece(h, xx):
        return out_ref.at[h, pl.ds(core * NT + xx * LQ, LQ)]

    for h in range(2):
        ag_copies.append(
            [
                remote(piece(h, x), piece(h, x), ag_s.at[h * X + dx], ag_r.at[h * X + dx], dev(xat(dx), c))
                for dx in range(1, X)
            ]
        )
        fx_copies.append(
            [
                remote(
                    piece(h, lax.rem(x - dx + X, X)), piece(h, lax.rem(x - dx + X, X)),
                    fx_s.at[h * X + dx], fx_r.at[h * X + dx], dev(x, c, 1 - core),
                )
                for dx in range(X)
            ]
        )

    def spread(h):
        @pl.when(jnp.logical_not(active(h, x)))
        def _():
            tot[h, X - 1] = jnp.zeros((LQ, B, B), f32)

        for dx in range(1, X):
            @pl.when(active(h, lax.rem(x - dx + X, X)))
            def _():
                xr_sends[h][dx].wait_recv()
                tot[h, X - 1] += xr[h, dx].astype(f32)

        for i in range(LQ):
            t = x * LQ + i
            n = pairs_of(lag_of(h, t), 0, nbr - 1)
            out_ref[h, core * NT + t] = (tot[h, X - 1, i] * (1.0 / jnp.maximum(n, 1.0))).astype(bf16)
        for cp in ag_copies[h]:
            cp.start()
        fx_copies[h][0].start()

    def gather(h):
        for dx in range(1, X):
            ag_copies[h][dx - 1].wait_recv()
            fx_copies[h][dx].start()

    def settle(h):
        for cp in fx_copies[h]:
            cp.wait_recv()
        for cp in ag_copies[h] + fx_copies[h]:
            cp.wait_send()

    for part in (spread, gather, settle):
        part(0)
        pl.when(has[1])(functools.partial(part, 1))

    @pl.when(jnp.logical_not(has[1]))
    def _():
        out_ref[1] = jnp.zeros((nb, B, B), bf16)

    for h in range(2):
        @pl.when(active(h, x))
        def _():
            for cp in tx_copies[h] + list(xr_sends[h].values()):
                cp.wait_send()

    for e in range(3):
        @pl.when(jnp.logical_not(om_self[e]))
        def _():
            om_copies[e].wait_send()

    for cp in pending:
        cp.wait_send()


def local(X, C, SDT, markov, omega):
    halves, nb = markov.shape[:2]
    NT = nb // 2
    PO, PQ, LQ = nb // C, NT // X, NT // X
    vmem, dma = pltpu.VMEM, pltpu.SemaphoreType.DMA
    scratch = [
        vmem((2, (nb + 2) * B, 2 * B), bf16),
        vmem((NT * KH, 2 * B), bf16),
        vmem((3, (NT + 2 * PQ - 2) * KH, 2 * B), bf16),
        vmem((2 * NT * KH, 2 * B), f32),
        vmem((2 * NT * KH, 2 * B), SDT),
        vmem((C, PO * KH, 2 * B), SDT),
        vmem((2, PO * KH, 2 * B), f32),
        vmem((KH, 4 * KH), f32),
        vmem((X, KH, 4 * KH), f32),
        vmem((KH, 4 * KH), f32),
        vmem((C, KH, 4 * KH), f32),
        vmem((2 * KH, 2 * KH), f32),
        vmem((4 * NT * KH, 2 * B), bf16),
        vmem((B, NT * B), bf16),
        vmem((NT * KH, 2 * B), f32),
        vmem((3, NT * KH, 2 * B), bf16),
        vmem((3 * X, PQ * KH, 2 * B), bf16),
        vmem((3, NT * KH, 2 * B), bf16),
        vmem((3 * NT, 2 * KH, 2 * B), bf16),
        vmem((2, X, LQ, B, B), f32),
        vmem((2, X, LQ, B, B), bf16),
        vmem((2, X, LQ, B, B), bf16),
        vmem((2, X, LQ, B, B), bf16),
        vmem((2, X, LQ, B, B), bf16),
        dma((4,)),
        dma((3,)), dma((3,)), dma((C,)), dma((C,)), dma, dma,
        dma((X,)), dma((X,)), dma((C,)), dma((C,)), dma((C,)), dma((C,)),
        dma((3 * X,)), dma((3 * X,)), dma((3 * X,)), dma((3 * X,)),
        *[dma((2 * X,))] * 8,
    ]
    excess = pl.pallas_call(
        functools.partial(kernel, X, C, nb, SDT),
        out_shape=jax.ShapeDtypeStruct((halves, nb, B, B), bf16),
        in_specs=[pl.BlockSpec(memory_space=pl.ANY), pl.BlockSpec(memory_space=pltpu.VMEM)],
        out_specs=pl.BlockSpec(memory_space=pltpu.VMEM),
        scratch_shapes=scratch,
        compiler_params=pltpu.CompilerParams(
            collective_id=0, has_side_effects=True, vmem_limit_bytes=48 * 2**20
        ),
        name="cadzow",
    )(markov.reshape(halves, nb * B, B), omega.T)
    lags = (
        jnp.arange(2, dtype=jnp.int32)[:, None] * (nb * C)
        + lax.axis_index("col") * nb
        + jnp.arange(nb, dtype=jnp.int32)[None, :]
    )
    counts = jnp.minimum(lags, 2 * nb * X - 1) - jnp.maximum(0, lags - nb * C + 1) + 1
    measured = markov.astype(f32)
    merged = 0.75 * measured + 0.5 * excess.astype(f32)
    return jnp.where((counts > 0)[:, :, None, None], merged, measured)


def solution(mesh):
    X, C = mesh.shape["row"] // 2, mesh.shape["col"]
    in_specs = (P(None, "col", None, None), P("col", None))
    return jax.shard_map(
        functools.partial(local, X, C, bf16),
        mesh=mesh,
        in_specs=in_specs,
        out_specs=P(None, "col", None, None),
        check_vma=False,
    )
```

```python
import functools

import jax
import jax.numpy as jnp
from jax import lax
from jax.experimental import pallas as pl
from jax.experimental.pallas import tpu as pltpu
from jax.sharding import PartitionSpec as P

NS_STEPS = 8
norm_floor = 1e-06
highest = lax.Precision.HIGHEST
MESH = pl.DeviceIdType.MESH
KH = 32
B = 128
f32, bf16 = jnp.float32, jnp.bfloat16
NT_DIMS = (((1,), (1,)), ((), ()))


def mm(left, right, **kw):
    return jnp.dot(left, right, preferred_element_type=f32, **kw)


def mm_nt(left, right, **kw):
    return lax.dot_general(left, right, NT_DIMS, preferred_element_type=f32, **kw)


def kernel(
    X, C, nb, SDT,
    l_ref, om_ref, out_ref,
    wl, q, omp, acc, s_send, s_recv, s_full, g_own, gx_recv, g_x, gc_recv, p_ref,
    bp, bpt, pacc, pr_send, pr_recv, prb, prx, tot, tx_send, tx_recv, ch, xr,
    sg, l_sem, om_s, om_r, s_s, s_r, sx_s, sx_r, sw_s, sw_r, gx_s, gx_r, gc_s, gc_r, b_s, b_r,
    pr_s, pr_r, pa_s, pa_r, tx_s, tx_r, xr_s, xr_r, ag_s, ag_r, fx_s, fx_r,
):
    NT = nb // 2
    HB = NT // 2
    PO = nb // C
    PQ = NT // X
    LQ = NT // X
    r = lax.axis_index("row")
    c = lax.axis_index("col")
    x, core = r // 2, r % 2

    def dev(xx, cc, kk=None):
        return (xx * 2 + (core if kk is None else kk), cc)

    def col(dc):
        return lax.rem(c + dc + 4 * C, C)

    def xat(dx):
        return lax.rem(x + dx, X)

    def xcol(dx, delta):
        xx = xat(dx)
        return dev(xx, lax.rem(c + 2 * (xx - x) + delta + 4 * C, C))

    def remote(src, dst, send, recv, device):
        return pltpu.make_async_remote_copy(
            src_ref=src, dst_ref=dst, send_sem=send, recv_sem=recv, device_id=device, device_id_type=MESH
        )

    halves = [jnp.where(c - 2 * x - e < 0, 1, 0).astype(jnp.int32) for e in range(3)]

    barrier = pltpu.get_barrier_semaphore()
    peers = [dev(x, col(dc)) for dc in range(1, C)]
    for dx in range(1, X):
        peers += [xcol(dx, delta) for delta in (-1, 0, 1)] + [dev(xat(dx), c)]
    peers.append(dev(x, c, 1 - core))
    for peer in peers:
        pl.semaphore_signal(barrier, inc=1, device_id=peer, device_id_type=MESH)

    loads = []
    for h in range(2):
        for s in range(2):
            loads.append(
                pltpu.make_async_copy(
                    l_ref.at[h],
                    wl.at[h, pl.ds((1 + s) * B, nb * B), pl.ds(s * B, B)],
                    l_sem.at[2 * h + s],
                )
            )
    for cp in loads:
        cp.start()
    half_rank = pl.ds(pl.multiple_of(core * KH, KH), KH)
    for w in range(NT):
        n = NT - 1 - w
        q[n * KH : (n + 1) * KH, :B] = om_ref[half_rank, (2 * w + 1) * B : (2 * w + 2) * B]
        q[n * KH : (n + 1) * KH, B:] = om_ref[half_rank, 2 * w * B : (2 * w + 1) * B]
    zero = jnp.zeros((B, B), bf16)
    for h in range(2):
        wl[h, 0:B, 0:B] = zero
        wl[h, 0:B, B:] = zero
        wl[h, B : 2 * B, B:] = zero
        wl[h, (nb + 1) * B :, 0:B] = zero
    bp[0 : NT * KH, :] = jnp.zeros((NT * KH, 2 * B), bf16)
    bp[3 * NT * KH :, :] = jnp.zeros((NT * KH, 2 * B), bf16)
    PAD = PQ - 1
    for e in range(3):
        omp[e, 0 : PAD * KH, :] = jnp.zeros((PAD * KH, 2 * B), bf16)
        omp[e, (PAD + NT) * KH :, :] = jnp.zeros((PAD * KH, 2 * B), bf16)
    pl.semaphore_wait(barrier, len(peers))

    pending = []

    om_self = [lax.rem(2 * x + e, C) == 0 for e in range(3)]
    om_copies = []
    for e in range(3):
        cp = remote(q, omp.at[e, pl.ds(PAD * KH, NT * KH)], om_s.at[e], om_r.at[e], dev(x, col(2 * x + e)))
        om_copies.append(cp)

        @pl.when(jnp.logical_not(om_self[e]))
        def _():
            cp.start()

        @pl.when(om_self[e])
        def _():
            omp[e, PAD * KH : (PAD + NT) * KH, :] = q[...]

    for cp in loads:
        cp.wait()

    def lags(e, tau):
        return wl[halves[e], tau * 2 * B : (tau + 1) * 2 * B, :]

    srows, brows = PO * KH, PQ * KH
    s_copies = []

    def send_sketch(first, last):
        for dst in range(first, last):
            dc = lax.rem(dst - c + C, C)
            cp = remote(
                s_send.at[pl.ds(dst * srows, srows)], s_recv.at[dc], s_s.at[dc], s_r.at[dc], dev(x, dst)
            )
            pl.when(dst != c)(cp.start)

    started = set()
    for e in range(3):
        @pl.when(jnp.logical_not(om_self[e]))
        def _():
            om_copies[e].wait_recv()

        for b in range(0, 2 * NT, PQ):
            value = None
            for tau in range(NT + 1):
                n = b + NT - tau - e * NT
                if -PQ < n < NT:
                    left = omp[e, (PAD + n) * KH : (PAD + n) * KH + brows, :]
                    term = mm_nt(left, lags(e, tau))
                    value = term if value is None else value + term
            if value is None:
                continue
            rows = slice(b * KH, b * KH + brows)
            if b in started:
                value = value + acc[rows, :]
            started.add(b)
            acc[rows, :] = value
            if (e == 1 and b < NT) or e == 2:
                s_send[rows, :] = value.astype(SDT)
        if e > 0:
            send_sketch((e - 1) * C // 2, e * C // 2)

    for dc in range(1, C):
        s_copies.append(
            remote(s_send.at[pl.ds(0, srows)], s_recv.at[dc], s_s.at[dc], s_r.at[dc], dev(x, col(dc)))
        )
    total = acc[pl.ds(pl.multiple_of(c * srows, srows), srows), :]
    for dc in range(1, C):
        s_copies[dc - 1].wait_recv()
        total = total + s_recv[dc].astype(f32)
    pending += s_copies
    s_full[core] = total
    over = remote(s_full.at[core], s_full.at[core], sx_s, sx_r, dev(x, c, 1 - core))
    over.start()
    mine = pl.ds(pl.multiple_of(c * srows, srows), srows)
    sg[core, mine, :] = total.astype(bf16)
    b_copies = []
    for dc in range(1, C):
        cp = remote(sg.at[core, mine], sg.at[core, mine], b_s.at[dc], b_r.at[dc], dev(x, col(dc)))
        cp.start()
        b_copies.append(cp)
    over.wait_recv()

    sk = jnp.concatenate(
        [
            jnp.concatenate([s_full[k, o * KH : (o + 1) * KH, :] for k in range(2)], axis=0)
            for o in range(PO)
        ],
        axis=1,
    )
    gram = mm_nt(sk, sk, precision=highest)
    g_own[...] = jnp.concatenate([gram[:KH], gram[KH:]], axis=1)
    gx_copies = []
    for dx in range(1, X):
        cp = remote(g_own, gx_recv.at[dx], gx_s.at[dx], gx_r.at[dx], dev(xat(dx), c))
        cp.start()
        gx_copies.append(cp)
    packed = g_own[...]
    for dx in range(1, X):
        gx_copies[dx - 1].wait_recv()
        packed = packed + gx_recv[dx]
    g_x[...] = packed
    gc_copies = []
    for dc in range(1, C):
        cp = remote(g_x, gc_recv.at[dc], gc_s.at[dc], gc_r.at[dc], dev(x, col(dc)))
        cp.start()
        gc_copies.append(cp)
    for cp in b_copies:
        cp.wait_recv()
    whole = remote(sg.at[core], sg.at[core], sw_s, sw_r, dev(x, c, 1 - core))
    whole.start()
    for dc in range(1, C):
        gc_copies[dc - 1].wait_recv()
        packed = packed + gc_recv[dc]
    pending += [over, *gx_copies, *b_copies, *gc_copies, whole]
    gram = jnp.concatenate([packed[:, : 2 * KH], packed[:, 2 * KH :]], axis=0)

    eye = (
        lax.broadcasted_iota(jnp.int32, (2 * KH, 2 * KH), 0)
        == lax.broadcasted_iota(jnp.int32, (2 * KH, 2 * KH), 1)
    ).astype(f32)
    trace = jnp.sum(gram * eye)
    scale = 1.0 / jnp.sqrt(jnp.full((1, 1), trace, f32) + norm_floor)
    inner = gram * (scale * scale)
    prod = None
    for sweep in range(NS_STEPS):
        a = 1.5 * eye - 0.5 * inner
        prod = a if prod is None else mm(prod, a, precision=highest)
        if sweep < NS_STEPS - 1:
            inner = mm(a, mm(inner, a, precision=highest), precision=highest)
    p_ref[...] = prod * scale
    weights = p_ref[half_rank, :]
    w1 = weights.astype(bf16)
    rest = weights - w1.astype(f32)
    w2 = rest.astype(bf16)
    w3 = (rest - w2.astype(f32)).astype(bf16)
    whole.wait_recv()
    stack = jnp.concatenate([w1, w2, w3], axis=0)
    for n in range(2 * NT):
        both = jnp.concatenate([sg[k, n * KH : (n + 1) * KH, :] for k in range(2)], axis=0)
        three = mm(stack, both)
        value = three[:KH] + three[KH : 2 * KH] + three[2 * KH :]
        bp[(NT + n) * KH : (NT + n + 1) * KH, :] = value.astype(bf16)

    qrows = PQ * KH
    pr_copies = {}
    for dx in range(X):
        for e in range(3):
            if dx > 0 or e != 1:
                slot = dx * 3 + e
                pr_copies[slot] = remote(
                    pr_send.at[e, pl.ds(0, qrows)], pr_recv.at[slot], pr_s.at[slot], pr_r.at[slot],
                    xcol(dx, 1 - e),
                )
    for e in (0, 2, 1):
        for b in range(0, NT, PQ):
            value = None
            for tau in range(NT + 1):
                if (e == 0 and b + PQ - 1 < NT - tau) or (e == 2 and b >= NT - tau):
                    continue
                first = (e * NT + b + tau) * KH
                term = mm(bp[first : first + qrows, :], lags(e, tau))
                value = term if value is None else value + term
            rows = slice(b * KH, b * KH + qrows)
            pr_send[e, rows, :] = value.astype(bf16)
            if e == 1:
                pacc[rows, :] = value
            owner = b // PQ
            dx = lax.rem(owner - x + X, X)
            slot = dx * 3 + e
            cp = remote(
                pr_send.at[e, pl.ds(b * KH, qrows)], pr_recv.at[slot], pr_s.at[slot], pr_r.at[slot],
                dev(owner, lax.rem(c + 2 * (owner - x) + 1 - e + 4 * C, C)),
            )
            if e == 1:
                pl.when(owner != x)(cp.start)
            else:
                cp.start()

    for g in range(NT):
        first = (NT + 2 * g) * KH
        pieces = [
            bp[first + o * KH : first + (o + 1) * KH, s * B : (s + 1) * B] for o in range(2) for s in range(2)
        ]
        bpt[:, g * B : (g + 1) * B] = jnp.concatenate(pieces, axis=0).T

    quarter = pl.ds(pl.multiple_of(x * qrows, qrows), qrows)
    total = pacc[quarter, :]
    for slot, cp in pr_copies.items():
        cp.wait_recv()
        total = total + pr_recv[slot].astype(f32)
    pending += list(pr_copies.values())
    prb[1, quarter, :] = total.astype(bf16)
    copies = []
    for dx in range(X):
        for e in range(3):
            if dx == 0 and e == 1:
                continue
            slot = dx * 3 + e
            cp = remote(
                prb.at[1, quarter], prb.at[e, quarter], pa_s.at[slot], pa_r.at[slot], xcol(dx, e - 1)
            )
            cp.start()
            copies.append(cp)
    for cp in copies:
        cp.wait_recv()
    pending += copies

    def active(h, xx):
        return c - 2 * xx >= 0 if h == 0 else c - 2 * xx - 2 < 0

    nbr, nbc = 2 * nb * X, nb * C

    def lag_of(h, t):
        return h * nbc + c * nb + core * NT + t

    def pairs_of(lag, first, last):
        low = jnp.maximum(first, lag - (nbc - 1))
        return jnp.maximum(jnp.minimum(last, lag) - low + 1, 0).astype(f32)

    def measured(h, t):
        return wl[h, pl.ds(pl.multiple_of((core * NT + t + 1) * B, B), B), 0:B].astype(f32)

    order = sorted(range(1, X), key=lambda dx: -min(dx, X - dx)) + [0]
    tx_copies, xr_sends = [], []
    for h in range(2):
        across, sends = [], {}
        for k, dx in enumerate(order):
            across.append(
                remote(
                    tx_send.at[h, k], tx_recv.at[h, k], tx_s.at[h * X + k], tx_r.at[h * X + k],
                    dev(x, c, 1 - core),
                )
            )
            if dx > 0:
                sends[dx] = remote(
                    ch.at[h, k], xr.at[h, dx], xr_s.at[h * X + dx], xr_r.at[h * X + dx], dev(xat(dx), c)
                )
        tx_copies.append(across)
        xr_sends.append(sends)

        @pl.when(active(h, x))
        def _():
            for e in range(3):
                @pl.when(halves[e] == h)
                def _():
                    for i in range(NT):
                        n = e * NT + i
                        pair = prb[e, i * KH : (i + 1) * KH, :]
                        prx[n, 0:KH, :] = pair
                        prx[n, KH:, :B] = pair[:, B:]
                        if n > 0:
                            prx[n - 1, KH:, B:] = pair[:, :B]

                @pl.when(halves[e] != h)
                def _():
                    for i in range(NT):
                        n = e * NT + i
                        prx[n, 0:KH, :] = jnp.zeros((KH, 2 * B), bf16)
                        prx[n, KH:, :B] = jnp.zeros((KH, B), bf16)
                        if n > 0:
                            prx[n - 1, KH:, B:] = jnp.zeros((KH, B), bf16)

            def lag_pair(tp):
                right = prx[pl.ds(NT - 1 - tp, 2 * NT)].reshape(4 * NT * KH, 2 * B)
                return mm(bpt[...], right)

            def combine(k):
                dx = order[k]
                across[k].wait_recv()
                for i in range(LQ):
                    t = xat(dx) * LQ + i
                    n = pairs_of(lag_of(h, t), 2 * nb * x, 2 * nb * (x + 1) - 1)
                    value = tot[h, k, i] + tx_recv[h, k, i].astype(f32) - (0.5 * n) * measured(h, t)
                    if dx > 0:
                        ch[h, k, i] = value.astype(bf16)
                    else:
                        tot[h, k, i] = value
                if dx > 0:
                    sends[dx].start()

            for k, dx in enumerate(order):
                first = xat(dx) * (LQ // 2)
                for i in range(LQ // 2):
                    value = lag_pair((1 - core) * HB + first + i).astype(bf16)
                    tx_send[h, k, 2 * i] = value[:, B:]
                    tx_send[h, k, 2 * i + 1] = value[:, :B]
                across[k].start()
                for i in range(LQ // 2):
                    value = lag_pair(core * HB + first + i)
                    tot[h, k, 2 * i] = value[:, B:]
                    tot[h, k, 2 * i + 1] = value[:, :B]
                if k > 0:
                    combine(k - 1)
            combine(X - 1)

    has = [None, c < 2 * X]
    ag_copies, fx_copies = [], []

    def piece(h, xx):
        return out_ref.at[h, pl.ds(core * NT + xx * LQ, LQ)]

    for h in range(2):
        ag_copies.append(
            [
                remote(piece(h, x), piece(h, x), ag_s.at[h * X + dx], ag_r.at[h * X + dx], dev(xat(dx), c))
                for dx in range(1, X)
            ]
        )
        fx_copies.append(
            [
                remote(
                    piece(h, lax.rem(x - dx + X, X)), piece(h, lax.rem(x - dx + X, X)),
                    fx_s.at[h * X + dx], fx_r.at[h * X + dx], dev(x, c, 1 - core),
                )
                for dx in range(X)
            ]
        )

    def spread(h):
        @pl.when(jnp.logical_not(active(h, x)))
        def _():
            tot[h, X - 1] = jnp.zeros((LQ, B, B), f32)

        for dx in range(1, X):
            @pl.when(active(h, lax.rem(x - dx + X, X)))
            def _():
                xr_sends[h][dx].wait_recv()
                tot[h, X - 1] += xr[h, dx].astype(f32)

        for i in range(LQ):
            t = x * LQ + i
            n = pairs_of(lag_of(h, t), 0, nbr - 1)
            out_ref[h, core * NT + t] = (tot[h, X - 1, i] * (1.0 / jnp.maximum(n, 1.0))).astype(bf16)
        for cp in ag_copies[h]:
            cp.start()
        fx_copies[h][0].start()

    def gather(h):
        for dx in range(1, X):
            ag_copies[h][dx - 1].wait_recv()
            fx_copies[h][dx].start()

    def settle(h):
        for cp in fx_copies[h]:
            cp.wait_recv()
        for cp in ag_copies[h] + fx_copies[h]:
            cp.wait_send()

    for part in (spread, gather, settle):
        part(0)
        pl.when(has[1])(functools.partial(part, 1))

    @pl.when(jnp.logical_not(has[1]))
    def _():
        out_ref[1] = jnp.zeros((nb, B, B), bf16)

    for h in range(2):
        @pl.when(active(h, x))
        def _():
            for cp in tx_copies[h] + list(xr_sends[h].values()):
                cp.wait_send()

    for e in range(3):
        @pl.when(jnp.logical_not(om_self[e]))
        def _():
            om_copies[e].wait_send()

    for cp in pending:
        cp.wait_send()


def local(X, C, SDT, markov, omega):
    halves, nb = markov.shape[:2]
    NT = nb // 2
    PO, PQ, LQ = nb // C, NT // X, NT // X
    vmem, dma = pltpu.VMEM, pltpu.SemaphoreType.DMA
    scratch = [
        vmem((2, (nb + 2) * B, 2 * B), bf16),
        vmem((NT * KH, 2 * B), bf16),
        vmem((3, (NT + 2 * PQ - 2) * KH, 2 * B), bf16),
        vmem((2 * NT * KH, 2 * B), f32),
        vmem((2 * NT * KH, 2 * B), SDT),
        vmem((C, PO * KH, 2 * B), SDT),
        vmem((2, PO * KH, 2 * B), f32),
        vmem((KH, 4 * KH), f32),
        vmem((X, KH, 4 * KH), f32),
        vmem((KH, 4 * KH), f32),
        vmem((C, KH, 4 * KH), f32),
        vmem((2 * KH, 2 * KH), f32),
        vmem((4 * NT * KH, 2 * B), bf16),
        vmem((B, NT * B), bf16),
        vmem((NT * KH, 2 * B), f32),
        vmem((3, NT * KH, 2 * B), bf16),
        vmem((3 * X, PQ * KH, 2 * B), bf16),
        vmem((3, NT * KH, 2 * B), bf16),
        vmem((3 * NT, 2 * KH, 2 * B), bf16),
        vmem((2, X, LQ, B, B), f32),
        vmem((2, X, LQ, B, B), bf16),
        vmem((2, X, LQ, B, B), bf16),
        vmem((2, X, LQ, B, B), bf16),
        vmem((2, X, LQ, B, B), bf16),
        vmem((2, 2 * NT * KH, 2 * B), bf16),
        dma((4,)),
        dma((3,)), dma((3,)), dma((C,)), dma((C,)), dma, dma, dma, dma,
        dma((X,)), dma((X,)), dma((C,)), dma((C,)), dma((C,)), dma((C,)),
        dma((3 * X,)), dma((3 * X,)), dma((3 * X,)), dma((3 * X,)),
        *[dma((2 * X,))] * 8,
    ]
    excess = pl.pallas_call(
        functools.partial(kernel, X, C, nb, SDT),
        out_shape=jax.ShapeDtypeStruct((halves, nb, B, B), bf16),
        in_specs=[pl.BlockSpec(memory_space=pl.ANY), pl.BlockSpec(memory_space=pltpu.VMEM)],
        out_specs=pl.BlockSpec(memory_space=pltpu.VMEM),
        scratch_shapes=scratch,
        compiler_params=pltpu.CompilerParams(
            collective_id=0, has_side_effects=True, vmem_limit_bytes=48 * 2**20
        ),
        name="cadzow",
    )(markov.reshape(halves, nb * B, B), omega.T)
    lags = (
        jnp.arange(2, dtype=jnp.int32)[:, None] * (nb * C)
        + lax.axis_index("col") * nb
        + jnp.arange(nb, dtype=jnp.int32)[None, :]
    )
    counts = jnp.minimum(lags, 2 * nb * X - 1) - jnp.maximum(0, lags - nb * C + 1) + 1
    measured = markov.astype(f32)
    merged = 0.75 * measured + 0.5 * excess.astype(f32)
    return jnp.where((counts > 0)[:, :, None, None], merged, measured)


def solution(mesh):
    X, C = mesh.shape["row"] // 2, mesh.shape["col"]
    in_specs = (P(None, "col", None, None), P("col", None))
    return jax.shard_map(
        functools.partial(local, X, C, bf16),
        mesh=mesh,
        in_specs=in_specs,
        out_specs=P(None, "col", None, None),
        check_vma=False,
    )
```

```python
import functools

import jax
import jax.numpy as jnp
from jax import lax
from jax.experimental import pallas as pl
from jax.experimental.pallas import tpu as pltpu
from jax.sharding import PartitionSpec as P

NS_STEPS = 8
norm_floor = 1e-06
highest = lax.Precision.HIGHEST
MESH = pl.DeviceIdType.MESH
KH = 32
B = 128
f32, bf16 = jnp.float32, jnp.bfloat16
NT_DIMS = (((1,), (1,)), ((), ()))


def mm(left, right, **kw):
    return jnp.dot(left, right, preferred_element_type=f32, **kw)


def mm_nt(left, right, **kw):
    return lax.dot_general(left, right, NT_DIMS, preferred_element_type=f32, **kw)


def kernel(
    X, C, nb, SDT,
    l_ref, om_ref, out_ref,
    wl, q, omp, acc, s_send, s_recv, g_own, gx_recv, p_ref,
    bp, bpt, pacc, pr_send, pr_recv, prb, prx, tot, tx_send, tx_recv, ch, xr,
    sg, om, l_sem, om_sem, om_s, om_r, s_s, s_r, sw_s, sw_r, gx_s, gx_r, b_s, b_r,
    pr_s, pr_r, pa_s, pa_r, tx_s, tx_r, xr_s, xr_r, ag_s, ag_r, fx_s, fx_r,
):
    NT = nb // 2
    HB = NT // 2
    PO = nb // C
    PQ = NT // X
    LQ = NT // X
    r = lax.axis_index("row")
    c = lax.axis_index("col")
    x, core = r // 2, r % 2

    def dev(xx, cc, kk=None):
        return (xx * 2 + (core if kk is None else kk), cc)

    def col(dc):
        return lax.rem(c + dc + 4 * C, C)

    def xat(dx):
        return lax.rem(x + dx, X)

    def xcol(dx, delta):
        xx = xat(dx)
        return dev(xx, lax.rem(c + 2 * (xx - x) + delta + 4 * C, C))

    def remote(src, dst, send, recv, device):
        return pltpu.make_async_remote_copy(
            src_ref=src, dst_ref=dst, send_sem=send, recv_sem=recv, device_id=device, device_id_type=MESH
        )

    halves = [jnp.where(c - 2 * x - e < 0, 1, 0).astype(jnp.int32) for e in range(3)]

    barrier = pltpu.get_barrier_semaphore()
    peers = [dev(x, col(dc)) for dc in range(1, C)]
    for dx in range(1, X):
        peers += [xcol(dx, delta) for delta in (-1, 0, 1)] + [dev(xat(dx), c)]
    peers.append(dev(x, c, 1 - core))
    for peer in peers:
        pl.semaphore_signal(barrier, inc=1, device_id=peer, device_id_type=MESH)

    loads = []
    for h in range(2):
        for s in range(2):
            loads.append(
                pltpu.make_async_copy(
                    l_ref.at[h],
                    wl.at[h, pl.ds((1 + s) * B, nb * B), pl.ds(s * B, B)],
                    l_sem.at[2 * h + s],
                )
            )
    for cp in loads:
        cp.start()
    half_rank = pl.ds(pl.multiple_of(core * KH, KH), KH)
    om_load = pltpu.make_async_copy(om_ref.at[half_rank], om, om_sem)
    om_load.start()
    zero = jnp.zeros((B, B), bf16)
    for h in range(2):
        wl[h, 0:B, 0:B] = zero
        wl[h, 0:B, B:] = zero
        wl[h, B : 2 * B, B:] = zero
        wl[h, (nb + 1) * B :, 0:B] = zero
    bp[0 : NT * KH, :] = jnp.zeros((NT * KH, 2 * B), bf16)
    bp[3 * NT * KH :, :] = jnp.zeros((NT * KH, 2 * B), bf16)
    PAD = PQ - 1
    for e in range(3):
        omp[e, 0 : PAD * KH, :] = jnp.zeros((PAD * KH, 2 * B), bf16)
        omp[e, (PAD + NT) * KH :, :] = jnp.zeros((PAD * KH, 2 * B), bf16)
    om_load.wait()
    for w in range(NT):
        n = NT - 1 - w
        q[n * KH : (n + 1) * KH, :B] = om[:, (2 * w + 1) * B : (2 * w + 2) * B]
        q[n * KH : (n + 1) * KH, B:] = om[:, 2 * w * B : (2 * w + 1) * B]
    pl.semaphore_wait(barrier, len(peers))

    pending = []

    om_self = [lax.rem(2 * x + e, C) == 0 for e in range(3)]
    om_copies = []
    for e in range(3):
        cp = remote(q, omp.at[e, pl.ds(PAD * KH, NT * KH)], om_s.at[e], om_r.at[e], dev(x, col(2 * x + e)))
        om_copies.append(cp)

        @pl.when(jnp.logical_not(om_self[e]))
        def _():
            cp.start()

        @pl.when(om_self[e])
        def _():
            omp[e, PAD * KH : (PAD + NT) * KH, :] = q[...]

    for cp in loads:
        cp.wait()

    def lags(e, tau):
        return wl[halves[e], tau * 2 * B : (tau + 1) * 2 * B, :]

    srows, brows = PO * KH, PQ * KH
    s_copies = []

    def send_sketch(first, last):
        for dst in range(first, last):
            dc = lax.rem(dst - c + C, C)
            cp = remote(
                s_send.at[pl.ds(dst * srows, srows)], s_recv.at[dc], s_s.at[dc], s_r.at[dc], dev(x, dst)
            )
            pl.when(dst != c)(cp.start)

    started = set()
    for e in range(3):
        @pl.when(jnp.logical_not(om_self[e]))
        def _():
            om_copies[e].wait_recv()

        for b in range(0, 2 * NT, PQ):
            value = None
            for tau in range(NT + 1):
                n = b + NT - tau - e * NT
                if -PQ < n < NT:
                    left = omp[e, (PAD + n) * KH : (PAD + n) * KH + brows, :]
                    term = mm_nt(left, lags(e, tau))
                    value = term if value is None else value + term
            if value is None:
                continue
            rows = slice(b * KH, b * KH + brows)
            if b in started:
                value = value + acc[rows, :]
            started.add(b)
            acc[rows, :] = value
            if (e == 1 and b < NT) or e == 2:
                s_send[rows, :] = value.astype(SDT)
        if e > 0:
            send_sketch((e - 1) * C // 2, e * C // 2)

    for dc in range(1, C):
        s_copies.append(
            remote(s_send.at[pl.ds(0, srows)], s_recv.at[dc], s_s.at[dc], s_r.at[dc], dev(x, col(dc)))
        )
    total = acc[pl.ds(pl.multiple_of(c * srows, srows), srows), :]
    for dc in range(1, C):
        s_copies[dc - 1].wait_recv()
        total = total + s_recv[dc].astype(f32)
    pending += s_copies
    mine = pl.ds(pl.multiple_of(c * srows, srows), srows)
    sg[core, mine, :] = total.astype(bf16)
    b_copies = {}
    side = 4 if C % 4 == 0 else 1

    def hops(dc):
        y, z = dc % side, dc // side
        return min(y, side - y) + min(z, C // side - z)

    for dc in sorted(range(1, C), key=lambda dc: -hops(dc)):
        b_copies[dc] = remote(sg.at[core, mine], sg.at[core, mine], b_s.at[dc], b_r.at[dc], dev(x, col(dc)))
        b_copies[dc].start()

    def row_pair(n):
        return jnp.concatenate(
            [sg[k, pl.ds(pl.multiple_of(n * KH, KH), KH), :] for k in range(2)], axis=0
        )

    groups = C // side
    group = [lax.rem(c // side + g, groups) for g in range(groups)]
    grows = side * srows
    overs = []
    for g in range(groups):
        for y in range(side):
            dc = lax.rem(c - (group[g] * side + y) + C, C)
            cp = remote(sg.at[core, mine], sg.at[core, mine], b_s.at[dc], b_r.at[dc], dev(x, c, 1 - core))
            pl.when(dc != 0)(cp.wait_recv)
        at = sg.at[core, pl.ds(pl.multiple_of(group[g] * grows, grows), grows)]
        overs.append(remote(at, at, sw_s.at[g], sw_r.at[g], dev(x, c, 1 - core)))
        overs[g].start()
    gram = None
    for g in range(groups):
        overs[g].wait_recv()
        for i in range(side * PO):
            both = row_pair(group[g] * (side * PO) + i)
            term = mm_nt(both, both)
            gram = term if gram is None else gram + term
    g_own[...] = jnp.concatenate([gram[:KH], gram[KH:]], axis=1)
    gx_copies = []
    for dx in range(1, X):
        cp = remote(g_own, gx_recv.at[dx], gx_s.at[dx], gx_r.at[dx], dev(xat(dx), c))
        cp.start()
        gx_copies.append(cp)
    packed = g_own[...]
    for dx in range(1, X):
        gx_copies[dx - 1].wait_recv()
        packed = packed + gx_recv[dx]
    pending += [*b_copies.values(), *overs, *gx_copies]
    gram = jnp.concatenate([packed[:, : 2 * KH], packed[:, 2 * KH :]], axis=0)

    eye = (
        lax.broadcasted_iota(jnp.int32, (2 * KH, 2 * KH), 0)
        == lax.broadcasted_iota(jnp.int32, (2 * KH, 2 * KH), 1)
    ).astype(f32)
    trace = jnp.sum(gram * eye)
    scale = 1.0 / jnp.sqrt(jnp.full((1, 1), trace, f32) + norm_floor)
    inner = gram * (scale * scale)
    prod = None
    for sweep in range(NS_STEPS):
        a = 1.5 * eye - 0.5 * inner
        prod = a if prod is None else mm(prod, a, precision=highest)
        if sweep < NS_STEPS - 1:
            inner = mm(a, mm(inner, a, precision=highest), precision=highest)
    p_ref[...] = prod * scale
    weights = p_ref[half_rank, :]
    w1 = weights.astype(bf16)
    rest = weights - w1.astype(f32)
    w2 = rest.astype(bf16)
    w3 = (rest - w2.astype(f32)).astype(bf16)
    stack = jnp.concatenate([w1, w2, w3], axis=0)
    for n in range(2 * NT):
        three = mm(stack, row_pair(n))
        value = three[:KH] + three[KH : 2 * KH] + three[2 * KH :]
        bp[(NT + n) * KH : (NT + n + 1) * KH, :] = value.astype(bf16)

    qrows = PQ * KH
    pr_copies = {}
    for dx in range(X):
        for e in range(3):
            if dx > 0 or e != 1:
                slot = dx * 3 + e
                pr_copies[slot] = remote(
                    pr_send.at[e, pl.ds(0, qrows)], pr_recv.at[slot], pr_s.at[slot], pr_r.at[slot],
                    xcol(dx, 1 - e),
                )
    for e in (0, 2, 1):
        for b in range(0, NT, PQ):
            value = None
            for tau in range(NT + 1):
                if (e == 0 and b + PQ - 1 < NT - tau) or (e == 2 and b >= NT - tau):
                    continue
                first = (e * NT + b + tau) * KH
                term = mm(bp[first : first + qrows, :], lags(e, tau))
                value = term if value is None else value + term
            rows = slice(b * KH, b * KH + qrows)
            pr_send[e, rows, :] = value.astype(bf16)
            if e == 1:
                pacc[rows, :] = value
            owner = b // PQ
            dx = lax.rem(owner - x + X, X)
            slot = dx * 3 + e
            cp = remote(
                pr_send.at[e, pl.ds(b * KH, qrows)], pr_recv.at[slot], pr_s.at[slot], pr_r.at[slot],
                dev(owner, lax.rem(c + 2 * (owner - x) + 1 - e + 4 * C, C)),
            )
            if e == 1:
                pl.when(owner != x)(cp.start)
            else:
                cp.start()

    for g in range(NT):
        first = (NT + 2 * g) * KH
        pieces = [
            bp[first + o * KH : first + (o + 1) * KH, s * B : (s + 1) * B] for o in range(2) for s in range(2)
        ]
        bpt[:, g * B : (g + 1) * B] = jnp.concatenate(pieces, axis=0).T

    quarter = pl.ds(pl.multiple_of(x * qrows, qrows), qrows)
    total = pacc[quarter, :]
    for slot, cp in pr_copies.items():
        cp.wait_recv()
        total = total + pr_recv[slot].astype(f32)
    pending += list(pr_copies.values())
    prb[1, quarter, :] = total.astype(bf16)
    copies = []
    for dx in sorted(range(X), key=lambda dx: -min(dx, X - dx)):
        for e in range(3):
            if dx == 0 and e == 1:
                continue
            slot = dx * 3 + e
            cp = remote(
                prb.at[1, quarter], prb.at[e, quarter], pa_s.at[slot], pa_r.at[slot], xcol(dx, e - 1)
            )
            cp.start()
            copies.append(cp)
    for cp in copies:
        cp.wait_recv()
    pending += copies

    def active(h, xx):
        return c - 2 * xx >= 0 if h == 0 else c - 2 * xx - 2 < 0

    nbr, nbc = 2 * nb * X, nb * C

    def lag_of(h, t):
        return h * nbc + c * nb + core * NT + t

    def pairs_of(lag, first, last):
        low = jnp.maximum(first, lag - (nbc - 1))
        return jnp.maximum(jnp.minimum(last, lag) - low + 1, 0).astype(f32)

    def measured(h, t):
        return wl[h, pl.ds(pl.multiple_of((core * NT + t + 1) * B, B), B), 0:B].astype(f32)

    order = sorted(range(1, X), key=lambda dx: -min(dx, X - dx)) + [0]
    tx_copies, xr_sends = [], []
    for h in range(2):
        across, sends = [], {}
        for k, dx in enumerate(order):
            across.append(
                remote(
                    tx_send.at[h, k], tx_recv.at[h, k], tx_s.at[h * X + k], tx_r.at[h * X + k],
                    dev(x, c, 1 - core),
                )
            )
            if dx > 0:
                sends[dx] = remote(
                    ch.at[h, k], xr.at[h, dx], xr_s.at[h * X + dx], xr_r.at[h * X + dx], dev(xat(dx), c)
                )
        tx_copies.append(across)
        xr_sends.append(sends)

        @pl.when(active(h, x))
        def _():
            for e in range(3):
                @pl.when(halves[e] == h)
                def _():
                    for i in range(NT):
                        n = e * NT + i
                        pair = prb[e, i * KH : (i + 1) * KH, :]
                        prx[n, 0:KH, :] = pair
                        prx[n, KH:, :B] = pair[:, B:]
                        if n > 0:
                            prx[n - 1, KH:, B:] = pair[:, :B]

                @pl.when(halves[e] != h)
                def _():
                    for i in range(NT):
                        n = e * NT + i
                        prx[n, 0:KH, :] = jnp.zeros((KH, 2 * B), bf16)
                        prx[n, KH:, :B] = jnp.zeros((KH, B), bf16)
                        if n > 0:
                            prx[n - 1, KH:, B:] = jnp.zeros((KH, B), bf16)

            def lag_pair(tp):
                right = prx[pl.ds(NT - 1 - tp, 2 * NT)].reshape(4 * NT * KH, 2 * B)
                return mm(bpt[...], right)

            def combine(k):
                dx = order[k]
                across[k].wait_recv()
                for i in range(LQ):
                    t = xat(dx) * LQ + i
                    n = pairs_of(lag_of(h, t), 2 * nb * x, 2 * nb * (x + 1) - 1)
                    value = tot[h, k, i] + tx_recv[h, k, i].astype(f32) - (0.5 * n) * measured(h, t)
                    if dx > 0:
                        ch[h, k, i] = value.astype(bf16)
                    else:
                        tot[h, k, i] = value
                if dx > 0:
                    sends[dx].start()

            for k, dx in enumerate(order):
                first = xat(dx) * (LQ // 2)
                for i in range(LQ // 2):
                    value = lag_pair((1 - core) * HB + first + i).astype(bf16)
                    tx_send[h, k, 2 * i] = value[:, B:]
                    tx_send[h, k, 2 * i + 1] = value[:, :B]
                across[k].start()
                for i in range(LQ // 2):
                    value = lag_pair(core * HB + first + i)
                    tot[h, k, 2 * i] = value[:, B:]
                    tot[h, k, 2 * i + 1] = value[:, :B]
                if k > 0:
                    combine(k - 1)
            combine(X - 1)

    has = [None, c < 2 * X]
    ag_copies, fx_copies = [], []

    def piece(h, xx):
        return out_ref.at[h, pl.ds(core * NT + xx * LQ, LQ)]

    for h in range(2):
        ag_copies.append(
            [
                remote(piece(h, x), piece(h, x), ag_s.at[h * X + dx], ag_r.at[h * X + dx], dev(xat(dx), c))
                for dx in range(1, X)
            ]
        )
        fx_copies.append(
            [
                remote(
                    piece(h, lax.rem(x - dx + X, X)), piece(h, lax.rem(x - dx + X, X)),
                    fx_s.at[h * X + dx], fx_r.at[h * X + dx], dev(x, c, 1 - core),
                )
                for dx in range(X)
            ]
        )

    def spread(h):
        @pl.when(jnp.logical_not(active(h, x)))
        def _():
            tot[h, X - 1] = jnp.zeros((LQ, B, B), f32)

        for dx in range(1, X):
            @pl.when(active(h, lax.rem(x - dx + X, X)))
            def _():
                xr_sends[h][dx].wait_recv()
                tot[h, X - 1] += xr[h, dx].astype(f32)

        for i in range(LQ):
            t = x * LQ + i
            n = pairs_of(lag_of(h, t), 0, nbr - 1)
            value = tot[h, X - 1, i] * (1.0 / jnp.maximum(n, 1.0))
            value = value + jnp.where(n > 0, 0.0, 0.5) * measured(h, t)
            out_ref[h, core * NT + t] = value.astype(bf16)
        for cp in ag_copies[h]:
            cp.start()
        fx_copies[h][0].start()

    def gather(h):
        for dx in range(1, X):
            ag_copies[h][dx - 1].wait_recv()
            fx_copies[h][dx].start()

    def settle(h):
        for cp in fx_copies[h]:
            cp.wait_recv()
        for cp in ag_copies[h] + fx_copies[h]:
            cp.wait_send()

    for part in (spread, gather, settle):
        part(0)
        pl.when(has[1])(functools.partial(part, 1))

    @pl.when(jnp.logical_not(has[1]))
    def _():
        for t in range(nb):
            out_ref[1, t] = (0.5 * wl[1, (t + 1) * B : (t + 2) * B, 0:B].astype(f32)).astype(bf16)

    for h in range(2):
        @pl.when(active(h, x))
        def _():
            for cp in tx_copies[h] + list(xr_sends[h].values()):
                cp.wait_send()

    for e in range(3):
        @pl.when(jnp.logical_not(om_self[e]))
        def _():
            om_copies[e].wait_send()

    for cp in pending:
        cp.wait_send()


def local(X, C, SDT, markov, omega):
    halves, nb = markov.shape[:2]
    NT = nb // 2
    PO, PQ, LQ = nb // C, NT // X, NT // X
    vmem, dma = pltpu.VMEM, pltpu.SemaphoreType.DMA
    scratch = [
        vmem((2, (nb + 2) * B, 2 * B), bf16),
        vmem((NT * KH, 2 * B), bf16),
        vmem((3, (NT + 2 * PQ - 2) * KH, 2 * B), bf16),
        vmem((2 * NT * KH, 2 * B), f32),
        vmem((2 * NT * KH, 2 * B), SDT),
        vmem((C, PO * KH, 2 * B), SDT),
        vmem((KH, 4 * KH), f32),
        vmem((X, KH, 4 * KH), f32),
        vmem((2 * KH, 2 * KH), f32),
        vmem((4 * NT * KH, 2 * B), bf16),
        vmem((B, NT * B), bf16),
        vmem((NT * KH, 2 * B), f32),
        vmem((3, NT * KH, 2 * B), bf16),
        vmem((3 * X, PQ * KH, 2 * B), bf16),
        vmem((3, NT * KH, 2 * B), bf16),
        vmem((3 * NT, 2 * KH, 2 * B), bf16),
        vmem((2, X, LQ, B, B), f32),
        vmem((2, X, LQ, B, B), bf16),
        vmem((2, X, LQ, B, B), bf16),
        vmem((2, X, LQ, B, B), bf16),
        vmem((2, X, LQ, B, B), bf16),
        vmem((2, 2 * NT * KH, 2 * B), bf16),
        vmem((KH, nb * B), bf16),
        dma((4,)), dma,
        dma((3,)), dma((3,)), dma((C,)), dma((C,)), dma((C,)), dma((C,)),
        dma((X,)), dma((X,)), dma((C,)), dma((C,)),
        dma((3 * X,)), dma((3 * X,)), dma((3 * X,)), dma((3 * X,)),
        *[dma((2 * X,))] * 8,
    ]
    excess = pl.pallas_call(
        functools.partial(kernel, X, C, nb, SDT),
        out_shape=pltpu.VMEM((halves, nb, B, B), bf16),
        in_specs=[pl.BlockSpec(memory_space=pltpu.HBM)] * 2,
        out_specs=pl.BlockSpec(memory_space=pltpu.VMEM),
        scratch_shapes=scratch,
        compiler_params=pltpu.CompilerParams(
            collective_id=0, has_side_effects=True, vmem_limit_bytes=57 * 2**20
        ),
        name="cadzow",
    )(markov.reshape(halves, nb * B, B), omega.T)
    return 0.75 * markov.astype(f32) + 0.5 * excess.astype(f32)


def solution(mesh):
    X, C = mesh.shape["row"] // 2, mesh.shape["col"]
    in_specs = (P(None, "col", None, None), P("col", None))
    return jax.shard_map(
        functools.partial(local, X, C, bf16),
        mesh=mesh,
        in_specs=in_specs,
        out_specs=P(None, "col", None, None),
        check_vma=False,
    )
```

```python
import functools

import jax
import jax.numpy as jnp
from jax import lax
from jax.experimental import pallas as pl
from jax.experimental.pallas import tpu as pltpu
from jax.sharding import PartitionSpec as P

NS_STEPS = 8
norm_floor = 1e-06
highest = lax.Precision.HIGHEST
MESH = pl.DeviceIdType.MESH
KH = 32
B = 128
f32, bf16 = jnp.float32, jnp.bfloat16
NT_DIMS = (((1,), (1,)), ((), ()))


def mm(left, right, **kw):
    return jnp.dot(left, right, preferred_element_type=f32, **kw)


def mm_nt(left, right, **kw):
    return lax.dot_general(left, right, NT_DIMS, preferred_element_type=f32, **kw)


def kernel(
    X, C, nb, SDT,
    l_ref, om_ref, out_ref,
    wl, q, omp, acc, s_send, s_recv, g_own, gx_recv, p_ref,
    bp, bpt, pacc, pr_send, pr_recv, prb, prx, tot, tx_send, tx_recv, ch, xr,
    sg, om, l_sem, om_sem, om_s, om_r, s_s, s_r, sw_s, sw_r, gx_s, gx_r, b_s, b_r,
    pr_s, pr_r, pa_s, pa_r, tx_s, tx_r, xr_s, xr_r, ag_s, ag_r, fx_s, fx_r,
):
    NT = nb // 2
    HB = NT // 2
    PO = nb // C
    PQ = NT // X
    LQ = NT // X
    r = lax.axis_index("row")
    c = lax.axis_index("col")
    x, core = r // 2, r % 2

    def dev(xx, cc, kk=None):
        return (xx * 2 + (core if kk is None else kk), cc)

    def col(dc):
        return lax.rem(c + dc + 4 * C, C)

    def xat(dx):
        return lax.rem(x + dx, X)

    def xcol(dx, delta):
        xx = xat(dx)
        return dev(xx, lax.rem(c + 2 * (xx - x) + delta + 4 * C, C))

    def remote(src, dst, send, recv, device):
        return pltpu.make_async_remote_copy(
            src_ref=src, dst_ref=dst, send_sem=send, recv_sem=recv, device_id=device, device_id_type=MESH
        )

    halves = [jnp.where(c - 2 * x - e < 0, 1, 0).astype(jnp.int32) for e in range(3)]

    barrier = pltpu.get_barrier_semaphore()
    side = 4 if C % 4 == 0 else 1

    def hops(dc):
        y, z = dc % side, dc // side
        return min(y, side - y) + min(z, C // side - z)

    far_cols = sorted(range(1, C), key=lambda dc: -hops(dc))
    far_x = sorted(range(1, X), key=lambda dx: -min(dx, X - dx))
    peers = [xcol(dx, delta) for dx in far_x for delta in (-1, 0, 1)]
    peers += [dev(x, col(dc)) for dc in far_cols]
    peers += [dev(xat(dx), c) for dx in far_x] + [dev(x, c, 1 - core)]
    for peer in peers:
        pl.semaphore_signal(barrier, inc=1, device_id=peer, device_id_type=MESH)

    loads = []
    for h in range(2):
        for s in range(2):
            loads.append(
                pltpu.make_async_copy(
                    l_ref.at[h],
                    wl.at[h, pl.ds((1 + s) * B, nb * B), pl.ds(s * B, B)],
                    l_sem.at[2 * h + s],
                )
            )
    for cp in loads:
        cp.start()
    half_rank = pl.ds(pl.multiple_of(core * KH, KH), KH)
    om_load = pltpu.make_async_copy(om_ref.at[half_rank], om, om_sem)
    om_load.start()
    zero = jnp.zeros((B, B), bf16)
    for h in range(2):
        wl[h, 0:B, 0:B] = zero
        wl[h, 0:B, B:] = zero
        wl[h, B : 2 * B, B:] = zero
        wl[h, (nb + 1) * B :, 0:B] = zero
    bp[0 : NT * KH, :] = jnp.zeros((NT * KH, 2 * B), bf16)
    bp[3 * NT * KH :, :] = jnp.zeros((NT * KH, 2 * B), bf16)
    PAD = PQ - 1
    for e in range(3):
        omp[e, 0 : PAD * KH, :] = jnp.zeros((PAD * KH, 2 * B), bf16)
        omp[e, (PAD + NT) * KH :, :] = jnp.zeros((PAD * KH, 2 * B), bf16)
    om_load.wait()
    for w in range(NT):
        n = NT - 1 - w
        q[n * KH : (n + 1) * KH, :B] = om[:, (2 * w + 1) * B : (2 * w + 2) * B]
        q[n * KH : (n + 1) * KH, B:] = om[:, 2 * w * B : (2 * w + 1) * B]
    pl.semaphore_wait(barrier, len(peers))

    pending = []

    om_self = [lax.rem(2 * x + e, C) == 0 for e in range(3)]
    om_copies = []
    for e in range(3):
        cp = remote(q, omp.at[e, pl.ds(PAD * KH, NT * KH)], om_s.at[e], om_r.at[e], dev(x, col(2 * x + e)))
        om_copies.append(cp)

        @pl.when(jnp.logical_not(om_self[e]))
        def _():
            cp.start()

        @pl.when(om_self[e])
        def _():
            omp[e, PAD * KH : (PAD + NT) * KH, :] = q[...]

    for cp in loads:
        cp.wait()

    def lags(e, tau):
        return wl[halves[e], tau * 2 * B : (tau + 1) * 2 * B, :]

    srows, brows = PO * KH, PQ * KH
    s_copies = []

    def send_sketch(first, last):
        for dst in range(first, last):
            dc = lax.rem(dst - c + C, C)
            cp = remote(
                s_send.at[pl.ds(dst * srows, srows)], s_recv.at[dc], s_s.at[dc], s_r.at[dc], dev(x, dst)
            )
            pl.when(dst != c)(cp.start)

    started = set()
    for e in range(3):
        @pl.when(jnp.logical_not(om_self[e]))
        def _():
            om_copies[e].wait_recv()

        for b in range(0, 2 * NT, PQ):
            value = None
            for tau in range(NT + 1):
                n = b + NT - tau - e * NT
                if -PQ < n < NT:
                    left = omp[e, (PAD + n) * KH : (PAD + n) * KH + brows, :]
                    term = mm_nt(left, lags(e, tau))
                    value = term if value is None else value + term
            if value is None:
                continue
            rows = slice(b * KH, b * KH + brows)
            if b in started:
                value = value + acc[rows, :]
            started.add(b)
            acc[rows, :] = value
            if (e == 1 and b < NT) or e == 2:
                s_send[rows, :] = value.astype(SDT)
        if e > 0:
            send_sketch((e - 1) * C // 2, e * C // 2)

    for dc in range(1, C):
        s_copies.append(
            remote(s_send.at[pl.ds(0, srows)], s_recv.at[dc], s_s.at[dc], s_r.at[dc], dev(x, col(dc)))
        )
    total = acc[pl.ds(pl.multiple_of(c * srows, srows), srows), :]
    for dc in range(1, C):
        s_copies[dc - 1].wait_recv()
        total = total + s_recv[dc].astype(f32)
    pending += s_copies
    mine = pl.ds(pl.multiple_of(c * srows, srows), srows)
    sg[core, mine, :] = total.astype(bf16)
    b_copies = {}
    for dc in far_cols:
        b_copies[dc] = remote(sg.at[core, mine], sg.at[core, mine], b_s.at[dc], b_r.at[dc], dev(x, col(dc)))
        b_copies[dc].start()

    def row_pair(n):
        return jnp.concatenate(
            [sg[k, pl.ds(pl.multiple_of(n * KH, KH), KH), :] for k in range(2)], axis=0
        )

    groups = C // side
    group = [lax.rem(c // side + g, groups) for g in range(groups)]
    grows = side * srows
    overs = []
    for g in range(groups):
        for y in range(side):
            dc = lax.rem(c - (group[g] * side + y) + C, C)
            cp = remote(sg.at[core, mine], sg.at[core, mine], b_s.at[dc], b_r.at[dc], dev(x, c, 1 - core))
            pl.when(dc != 0)(cp.wait_recv)
        at = sg.at[core, pl.ds(pl.multiple_of(group[g] * grows, grows), grows)]
        overs.append(remote(at, at, sw_s.at[g], sw_r.at[g], dev(x, c, 1 - core)))
        overs[g].start()
    gram = None
    for g in range(groups):
        overs[g].wait_recv()
        for i in range(side * PO):
            both = row_pair(group[g] * (side * PO) + i)
            term = mm_nt(both, both)
            gram = term if gram is None else gram + term
    g_own[...] = jnp.concatenate([gram[:KH], gram[KH:]], axis=1)
    gx_copies = []
    for dx in range(1, X):
        cp = remote(g_own, gx_recv.at[dx], gx_s.at[dx], gx_r.at[dx], dev(xat(dx), c))
        cp.start()
        gx_copies.append(cp)
    packed = g_own[...]
    for dx in range(1, X):
        gx_copies[dx - 1].wait_recv()
        packed = packed + gx_recv[dx]
    pending += [*b_copies.values(), *overs, *gx_copies]
    gram = jnp.concatenate([packed[:, : 2 * KH], packed[:, 2 * KH :]], axis=0)

    eye = (
        lax.broadcasted_iota(jnp.int32, (2 * KH, 2 * KH), 0)
        == lax.broadcasted_iota(jnp.int32, (2 * KH, 2 * KH), 1)
    ).astype(f32)
    trace = jnp.sum(gram * eye)
    scale = 1.0 / jnp.sqrt(jnp.full((1, 1), trace, f32) + norm_floor)
    inner = gram * (scale * scale)
    prod = None
    for sweep in range(NS_STEPS):
        a = 1.5 * eye - 0.5 * inner
        prod = a if prod is None else mm(prod, a, precision=highest)
        if sweep < NS_STEPS - 1:
            inner = mm(a, mm(inner, a, precision=highest), precision=highest)
    p_ref[...] = prod * scale
    weights = p_ref[half_rank, :]
    w1 = weights.astype(bf16)
    rest = weights - w1.astype(f32)
    w2 = rest.astype(bf16)
    w3 = (rest - w2.astype(f32)).astype(bf16)
    stack = jnp.concatenate([w1, w2, w3], axis=0)
    for n in range(2 * NT):
        three = mm(stack, row_pair(n))
        value = three[:KH] + three[KH : 2 * KH] + three[2 * KH :]
        bp[(NT + n) * KH : (NT + n + 1) * KH, :] = value.astype(bf16)

    qrows = PQ * KH
    pr_copies = {}
    for dx in range(X):
        for e in range(3):
            if dx > 0 or e != 1:
                slot = dx * 3 + e
                pr_copies[slot] = remote(
                    pr_send.at[e, pl.ds(0, qrows)], pr_recv.at[slot], pr_s.at[slot], pr_r.at[slot],
                    xcol(dx, 1 - e),
                )
    for e in (0, 2, 1):
        for b in range(0, NT, PQ):
            value = None
            for tau in range(NT + 1):
                if (e == 0 and b + PQ - 1 < NT - tau) or (e == 2 and b >= NT - tau):
                    continue
                first = (e * NT + b + tau) * KH
                term = mm(bp[first : first + qrows, :], lags(e, tau))
                value = term if value is None else value + term
            rows = slice(b * KH, b * KH + qrows)
            pr_send[e, rows, :] = value.astype(bf16)
            if e == 1:
                pacc[rows, :] = value
            owner = b // PQ
            dx = lax.rem(owner - x + X, X)
            slot = dx * 3 + e
            cp = remote(
                pr_send.at[e, pl.ds(b * KH, qrows)], pr_recv.at[slot], pr_s.at[slot], pr_r.at[slot],
                dev(owner, lax.rem(c + 2 * (owner - x) + 1 - e + 4 * C, C)),
            )
            if e == 1:
                pl.when(owner != x)(cp.start)
            else:
                cp.start()

    for g in range(NT):
        first = (NT + 2 * g) * KH
        pieces = [
            bp[first + o * KH : first + (o + 1) * KH, s * B : (s + 1) * B] for o in range(2) for s in range(2)
        ]
        bpt[:, g * B : (g + 1) * B] = jnp.concatenate(pieces, axis=0).T

    quarter = pl.ds(pl.multiple_of(x * qrows, qrows), qrows)
    total = pacc[quarter, :]
    for slot, cp in pr_copies.items():
        cp.wait_recv()
        total = total + pr_recv[slot].astype(f32)
    pending += list(pr_copies.values())
    prb[1, quarter, :] = total.astype(bf16)
    copies = []
    for dx in sorted(range(X), key=lambda dx: -min(dx, X - dx)):
        for e in range(3):
            if dx == 0 and e == 1:
                continue
            slot = dx * 3 + e
            cp = remote(
                prb.at[1, quarter], prb.at[e, quarter], pa_s.at[slot], pa_r.at[slot], xcol(dx, e - 1)
            )
            cp.start()
            copies.append(cp)
    for cp in copies:
        cp.wait_recv()
    pending += copies

    def active(h, xx):
        return c - 2 * xx >= 0 if h == 0 else c - 2 * xx - 2 < 0

    nbr, nbc = 2 * nb * X, nb * C

    def lag_of(h, t):
        return h * nbc + c * nb + core * NT + t

    def pairs_of(lag, first, last):
        low = jnp.maximum(first, lag - (nbc - 1))
        return jnp.maximum(jnp.minimum(last, lag) - low + 1, 0).astype(f32)

    def measured(h, t):
        return wl[h, pl.ds(pl.multiple_of((core * NT + t + 1) * B, B), B), 0:B].astype(f32)

    order = sorted(range(1, X), key=lambda dx: -min(dx, X - dx)) + [0]
    tx_copies, xr_sends = [], []
    for h in range(2):
        across, sends = [], {}
        for k, dx in enumerate(order):
            across.append(
                remote(
                    tx_send.at[h, k], tx_recv.at[h, k], tx_s.at[h * X + k], tx_r.at[h * X + k],
                    dev(x, c, 1 - core),
                )
            )
            if dx > 0:
                sends[dx] = remote(
                    ch.at[h, k], xr.at[h, dx], xr_s.at[h * X + dx], xr_r.at[h * X + dx], dev(xat(dx), c)
                )
        tx_copies.append(across)
        xr_sends.append(sends)

        @pl.when(active(h, x))
        def _():
            for e in range(3):
                @pl.when(halves[e] == h)
                def _():
                    for i in range(NT):
                        n = e * NT + i
                        pair = prb[e, i * KH : (i + 1) * KH, :]
                        prx[n, 0:KH, :] = pair
                        prx[n, KH:, :B] = pair[:, B:]
                        if n > 0:
                            prx[n - 1, KH:, B:] = pair[:, :B]

                @pl.when(halves[e] != h)
                def _():
                    for i in range(NT):
                        n = e * NT + i
                        prx[n, 0:KH, :] = jnp.zeros((KH, 2 * B), bf16)
                        prx[n, KH:, :B] = jnp.zeros((KH, B), bf16)
                        if n > 0:
                            prx[n - 1, KH:, B:] = jnp.zeros((KH, B), bf16)

            def lag_pair(tp, first, count):
                depth = 2 * NT * KH
                right = prx[pl.ds(NT - 1 - tp + first * NT, count * NT)].reshape(count * depth, 2 * B)
                return mm(bpt[:, first * depth : (first + count) * depth], right)

            def combine(k):
                dx = order[k]
                across[k].wait_recv()
                for i in range(LQ):
                    t = xat(dx) * LQ + i
                    n = pairs_of(lag_of(h, t), 2 * nb * x, 2 * nb * (x + 1) - 1)
                    value = tot[h, k, i] + tx_recv[h, k, i].astype(f32) - (0.5 * n) * measured(h, t)
                    if dx > 0:
                        ch[h, k, i] = value.astype(bf16)
                    else:
                        tot[h, k, i] = value
                if dx > 0:
                    sends[dx].start()

            def pipeline(*rows):
                for k, dx in enumerate(order):
                    first = xat(dx) * (LQ // 2)
                    for i in range(LQ // 2):
                        value = lag_pair((1 - core) * HB + first + i, *rows).astype(bf16)
                        tx_send[h, k, 2 * i] = value[:, B:]
                        tx_send[h, k, 2 * i + 1] = value[:, :B]
                    across[k].start()
                    for i in range(LQ // 2):
                        value = lag_pair(core * HB + first + i, *rows)
                        tot[h, k, 2 * i] = value[:, B:]
                        tot[h, k, 2 * i + 1] = value[:, :B]
                    if k > 0:
                        combine(k - 1)
                combine(X - 1)

            pl.when(halves[1] == h)(functools.partial(pipeline, 0, 2))
            pl.when(halves[1] != h)(functools.partial(pipeline, h, 1))

    has = [None, c < 2 * X]
    ag_copies, fx_copies = [], []

    def piece(h, xx):
        return out_ref.at[h, pl.ds(core * NT + xx * LQ, LQ)]

    for h in range(2):
        ag_copies.append(
            [
                remote(piece(h, x), piece(h, x), ag_s.at[h * X + dx], ag_r.at[h * X + dx], dev(xat(dx), c))
                for dx in range(1, X)
            ]
        )
        fx_copies.append(
            [
                remote(
                    piece(h, lax.rem(x - dx + X, X)), piece(h, lax.rem(x - dx + X, X)),
                    fx_s.at[h * X + dx], fx_r.at[h * X + dx], dev(x, c, 1 - core),
                )
                for dx in range(X)
            ]
        )

    def spread(h):
        @pl.when(jnp.logical_not(active(h, x)))
        def _():
            tot[h, X - 1] = jnp.zeros((LQ, B, B), f32)

        for dx in range(1, X):
            @pl.when(active(h, lax.rem(x - dx + X, X)))
            def _():
                xr_sends[h][dx].wait_recv()
                tot[h, X - 1] += xr[h, dx].astype(f32)

        for i in range(LQ):
            t = x * LQ + i
            n = pairs_of(lag_of(h, t), 0, nbr - 1)
            value = tot[h, X - 1, i] * (1.0 / jnp.maximum(n, 1.0))
            value = value + jnp.where(n > 0, 0.0, 0.5) * measured(h, t)
            out_ref[h, core * NT + t] = value.astype(bf16)
        for cp in ag_copies[h]:
            cp.start()
        fx_copies[h][0].start()

    def gather(h):
        for dx in range(1, X):
            ag_copies[h][dx - 1].wait_recv()
            fx_copies[h][dx].start()

    def settle(h):
        for cp in fx_copies[h]:
            cp.wait_recv()
        for cp in ag_copies[h] + fx_copies[h]:
            cp.wait_send()

    for part in (spread, gather, settle):
        part(0)
        pl.when(has[1])(functools.partial(part, 1))

    @pl.when(jnp.logical_not(has[1]))
    def _():
        for t in range(nb):
            out_ref[1, t] = (0.5 * wl[1, (t + 1) * B : (t + 2) * B, 0:B].astype(f32)).astype(bf16)

    for h in range(2):
        @pl.when(active(h, x))
        def _():
            for cp in tx_copies[h] + list(xr_sends[h].values()):
                cp.wait_send()

    for e in range(3):
        @pl.when(jnp.logical_not(om_self[e]))
        def _():
            om_copies[e].wait_send()

    for cp in pending:
        cp.wait_send()


def local(X, C, SDT, markov, omega):
    halves, nb = markov.shape[:2]
    NT = nb // 2
    PO, PQ, LQ = nb // C, NT // X, NT // X
    vmem, dma = pltpu.VMEM, pltpu.SemaphoreType.DMA
    scratch = [
        vmem((2, (nb + 2) * B, 2 * B), bf16),
        vmem((NT * KH, 2 * B), bf16),
        vmem((3, (NT + 2 * PQ - 2) * KH, 2 * B), bf16),
        vmem((2 * NT * KH, 2 * B), f32),
        vmem((2 * NT * KH, 2 * B), SDT),
        vmem((C, PO * KH, 2 * B), SDT),
        vmem((KH, 4 * KH), f32),
        vmem((X, KH, 4 * KH), f32),
        vmem((2 * KH, 2 * KH), f32),
        vmem((4 * NT * KH, 2 * B), bf16),
        vmem((B, NT * B), bf16),
        vmem((NT * KH, 2 * B), f32),
        vmem((3, NT * KH, 2 * B), bf16),
        vmem((3 * X, PQ * KH, 2 * B), bf16),
        vmem((3, NT * KH, 2 * B), bf16),
        vmem((3 * NT, 2 * KH, 2 * B), bf16),
        vmem((2, X, LQ, B, B), f32),
        vmem((2, X, LQ, B, B), bf16),
        vmem((2, X, LQ, B, B), bf16),
        vmem((2, X, LQ, B, B), bf16),
        vmem((2, X, LQ, B, B), bf16),
        vmem((2, 2 * NT * KH, 2 * B), bf16),
        vmem((KH, nb * B), bf16),
        dma((4,)), dma,
        dma((3,)), dma((3,)), dma((C,)), dma((C,)), dma((C,)), dma((C,)),
        dma((X,)), dma((X,)), dma((C,)), dma((C,)),
        dma((3 * X,)), dma((3 * X,)), dma((3 * X,)), dma((3 * X,)),
        *[dma((2 * X,))] * 8,
    ]
    excess = pl.pallas_call(
        functools.partial(kernel, X, C, nb, SDT),
        out_shape=pltpu.VMEM((halves, nb, B, B), bf16),
        in_specs=[pl.BlockSpec(memory_space=pltpu.HBM)] * 2,
        out_specs=pl.BlockSpec(memory_space=pltpu.VMEM),
        scratch_shapes=scratch,
        compiler_params=pltpu.CompilerParams(
            collective_id=0, has_side_effects=True, vmem_limit_bytes=57 * 2**20
        ),
        name="cadzow",
    )(markov.reshape(halves, nb * B, B), omega.T)
    return 0.75 * markov.astype(f32) + 0.5 * excess.astype(f32)


def solution(mesh):
    X, C = mesh.shape["row"] // 2, mesh.shape["col"]
    in_specs = (P(None, "col", None, None), P("col", None))
    return jax.shard_map(
        functools.partial(local, X, C, bf16),
        mesh=mesh,
        in_specs=in_specs,
        out_specs=P(None, "col", None, None),
        check_vma=False,
    )
```

```python
import functools

import jax
import jax.numpy as jnp
from jax import lax
from jax.experimental import pallas as pl
from jax.experimental.pallas import tpu as pltpu
from jax.sharding import PartitionSpec as P

NS_STEPS = 8
norm_floor = 1e-06
highest = lax.Precision.HIGHEST
MESH = pl.DeviceIdType.MESH
KH = 32
B = 128
f32, bf16 = jnp.float32, jnp.bfloat16
NT_DIMS = (((1,), (1,)), ((), ()))


def mm(left, right, **kw):
    return jnp.dot(left, right, preferred_element_type=f32, **kw)


def mm_nt(left, right, **kw):
    return lax.dot_general(left, right, NT_DIMS, preferred_element_type=f32, **kw)


def kernel(
    X, C, nb, SDT,
    l_ref, om_ref, out_ref,
    wl, q, omp, acc, s_send, s_recv, g_own, gx_recv, p_ref,
    bp, bpt, pacc, pr_send, pr_recv, prb, prx, tot, tx_send, tx_recv, ch, xr,
    sg, om, sp, rfull, rf_s, rf_r, l_sem, om_sem, om_s, om_r, s_s, s_r, sw_s, sw_r, gx_s, gx_r, b_s, b_r,
    pr_s, pr_r, pa_s, pa_r, tx_s, tx_r, xr_s, xr_r, ag_s, ag_r, fx_s, fx_r,
):
    NT = nb // 2
    HB = NT // 2
    PO = nb // C
    PQ = NT // X
    LQ = NT // X
    r = lax.axis_index("row")
    c = lax.axis_index("col")
    x, core = r // 2, r % 2

    def dev(xx, cc, kk=None):
        return (xx * 2 + (core if kk is None else kk), cc)

    def col(dc):
        return lax.rem(c + dc + 4 * C, C)

    def xat(dx):
        return lax.rem(x + dx, X)

    def xcol(dx, delta):
        xx = xat(dx)
        return dev(xx, lax.rem(c + 2 * (xx - x) + delta + 4 * C, C))

    def remote(src, dst, send, recv, device):
        return pltpu.make_async_remote_copy(
            src_ref=src, dst_ref=dst, send_sem=send, recv_sem=recv, device_id=device, device_id_type=MESH
        )

    halves = [jnp.where(c - 2 * x - e < 0, 1, 0).astype(jnp.int32) for e in range(3)]

    barrier = pltpu.get_barrier_semaphore()
    peers = [dev(x, col(dc)) for dc in range(1, C)]
    for dx in range(1, X):
        peers += [xcol(dx, delta) for delta in (-1, 0, 1)] + [dev(xat(dx), c)]
    peers.append(dev(x, c, 1 - core))
    for peer in peers:
        pl.semaphore_signal(barrier, inc=1, device_id=peer, device_id_type=MESH)

    loads = []
    for h in range(2):
        for s in range(2):
            loads.append(
                pltpu.make_async_copy(
                    l_ref.at[h],
                    wl.at[h, pl.ds((1 + s) * B, nb * B), pl.ds(s * B, B)],
                    l_sem.at[2 * h + s],
                )
            )
    for cp in loads:
        cp.start()
    half_rank = pl.ds(pl.multiple_of(core * KH, KH), KH)
    om_load = pltpu.make_async_copy(om_ref.at[half_rank], om, om_sem)
    om_load.start()
    zero = jnp.zeros((B, B), bf16)
    for h in range(2):
        wl[h, 0:B, 0:B] = zero
        wl[h, 0:B, B:] = zero
        wl[h, B : 2 * B, B:] = zero
        wl[h, (nb + 1) * B :, 0:B] = zero
    sp[0 : NT * KH, :] = jnp.zeros((NT * KH, 2 * B), bf16)
    sp[3 * NT * KH :, :] = jnp.zeros((NT * KH, 2 * B), bf16)
    PAD = PQ - 1
    for e in range(3):
        omp[e, 0 : PAD * KH, :] = jnp.zeros((PAD * KH, 2 * B), bf16)
        omp[e, (PAD + NT) * KH :, :] = jnp.zeros((PAD * KH, 2 * B), bf16)
    om_load.wait()
    for w in range(NT):
        n = NT - 1 - w
        q[n * KH : (n + 1) * KH, :B] = om[:, (2 * w + 1) * B : (2 * w + 2) * B]
        q[n * KH : (n + 1) * KH, B:] = om[:, 2 * w * B : (2 * w + 1) * B]
    pl.semaphore_wait(barrier, len(peers))

    pending = []

    om_self = [lax.rem(2 * x + e, C) == 0 for e in range(3)]
    om_copies = []
    for e in range(3):
        cp = remote(q, omp.at[e, pl.ds(PAD * KH, NT * KH)], om_s.at[e], om_r.at[e], dev(x, col(2 * x + e)))
        om_copies.append(cp)

        @pl.when(jnp.logical_not(om_self[e]))
        def _():
            cp.start()

        @pl.when(om_self[e])
        def _():
            omp[e, PAD * KH : (PAD + NT) * KH, :] = q[...]

    for cp in loads:
        cp.wait()

    def lags(e, tau):
        return wl[halves[e], tau * 2 * B : (tau + 1) * 2 * B, :]

    srows, brows = PO * KH, PQ * KH
    s_copies = []

    def send_sketch(first, last):
        for dst in range(first, last):
            dc = lax.rem(dst - c + C, C)
            cp = remote(
                s_send.at[pl.ds(dst * srows, srows)], s_recv.at[dc], s_s.at[dc], s_r.at[dc], dev(x, dst)
            )
            pl.when(dst != c)(cp.start)

    started = set()
    for e in range(3):
        @pl.when(jnp.logical_not(om_self[e]))
        def _():
            om_copies[e].wait_recv()

        for b in range(0, 2 * NT, PQ):
            value = None
            for tau in range(NT + 1):
                n = b + NT - tau - e * NT
                if -PQ < n < NT:
                    left = omp[e, (PAD + n) * KH : (PAD + n) * KH + brows, :]
                    term = mm_nt(left, lags(e, tau))
                    value = term if value is None else value + term
            if value is None:
                continue
            rows = slice(b * KH, b * KH + brows)
            if b in started:
                value = value + acc[rows, :]
            started.add(b)
            acc[rows, :] = value
            if (e == 1 and b < NT) or e == 2:
                s_send[rows, :] = value.astype(SDT)
        if e > 0:
            send_sketch((e - 1) * C // 2, e * C // 2)

    for dc in range(1, C):
        s_copies.append(
            remote(s_send.at[pl.ds(0, srows)], s_recv.at[dc], s_s.at[dc], s_r.at[dc], dev(x, col(dc)))
        )
    total = acc[pl.ds(pl.multiple_of(c * srows, srows), srows), :]
    for dc in range(1, C):
        s_copies[dc - 1].wait_recv()
        total = total + s_recv[dc].astype(f32)
    pending += s_copies
    mine = pl.ds(pl.multiple_of(c * srows, srows), srows)
    sg[core, mine, :] = total.astype(bf16)
    b_copies = {}
    side = 4 if C % 4 == 0 else 1

    def hops(dc):
        y, z = dc % side, dc // side
        return min(y, side - y) + min(z, C // side - z)

    for dc in sorted(range(1, C), key=lambda dc: -hops(dc)):
        b_copies[dc] = remote(sg.at[core, mine], sg.at[core, mine], b_s.at[dc], b_r.at[dc], dev(x, col(dc)))
        b_copies[dc].start()

    def row_pair(n):
        return jnp.concatenate(
            [sg[k, pl.ds(pl.multiple_of(n * KH, KH), KH), :] for k in range(2)], axis=0
        )

    groups = C // side
    group = [lax.rem(c // side + g, groups) for g in range(groups)]
    grows = side * srows
    overs = []
    for g in range(groups):
        for y in range(side):
            dc = lax.rem(c - (group[g] * side + y) + C, C)
            cp = remote(sg.at[core, mine], sg.at[core, mine], b_s.at[dc], b_r.at[dc], dev(x, c, 1 - core))
            pl.when(dc != 0)(cp.wait_recv)
        at = sg.at[core, pl.ds(pl.multiple_of(group[g] * grows, grows), grows)]
        overs.append(remote(at, at, sw_s.at[g], sw_r.at[g], dev(x, c, 1 - core)))
        overs[g].start()
    gram = None
    for g in range(groups):
        overs[g].wait_recv()
        for i in range(side * PO):
            both = row_pair(group[g] * (side * PO) + i)
            term = mm_nt(both, both)
            gram = term if gram is None else gram + term
    g_own[...] = jnp.concatenate([gram[:KH], gram[KH:]], axis=1)
    gx_copies = []
    for dx in range(1, X):
        cp = remote(g_own, gx_recv.at[dx], gx_s.at[dx], gx_r.at[dx], dev(xat(dx), c))
        cp.start()
        gx_copies.append(cp)
    sp[NT * KH : 3 * NT * KH, :] = sg[core]
    qrows = PQ * KH
    swaps = []
    for e in (0, 2, 1):
        for b in range(0, NT, PQ):
            value = None
            for tau in range(NT + 1):
                if (e == 0 and b + PQ - 1 < NT - tau) or (e == 2 and b >= NT - tau):
                    continue
                first = (e * NT + b + tau) * KH
                term = mm(sp[first : first + qrows, :], lags(e, tau))
                value = term if value is None else value + term
            rfull[core, e, b * KH : b * KH + qrows, :] = value
        at = rfull.at[core, e]
        cp = remote(at, at, rf_s.at[e], rf_r.at[e], dev(x, c, 1 - core))
        cp.start()
        swaps.append(cp)

    packed = g_own[...]
    for dx in range(1, X):
        gx_copies[dx - 1].wait_recv()
        packed = packed + gx_recv[dx]
    pending += [*b_copies.values(), *overs, *gx_copies, *swaps]
    gram = jnp.concatenate([packed[:, : 2 * KH], packed[:, 2 * KH :]], axis=0)

    eye = (
        lax.broadcasted_iota(jnp.int32, (2 * KH, 2 * KH), 0)
        == lax.broadcasted_iota(jnp.int32, (2 * KH, 2 * KH), 1)
    ).astype(f32)
    trace = jnp.sum(gram * eye)
    scale = 1.0 / jnp.sqrt(jnp.full((1, 1), trace, f32) + norm_floor)
    inner = gram * (scale * scale)
    prod = None
    for sweep in range(NS_STEPS):
        a = 1.5 * eye - 0.5 * inner
        prod = a if prod is None else mm(prod, a, precision=highest)
        if sweep < NS_STEPS - 1:
            inner = mm(a, mm(inner, a, precision=highest), precision=highest)
    p_ref[...] = prod * scale
    weights = p_ref[half_rank, :]
    w1 = weights.astype(bf16)
    rest = weights - w1.astype(f32)
    w2 = rest.astype(bf16)
    w3 = (rest - w2.astype(f32)).astype(bf16)
    stack = jnp.concatenate([w1, w2, w3], axis=0)

    pr_copies = {}
    for dx in range(X):
        for e in range(3):
            if dx > 0 or e != 1:
                slot = dx * 3 + e
                pr_copies[slot] = remote(
                    pr_send.at[e, pl.ds(0, qrows)], pr_recv.at[slot], pr_s.at[slot], pr_r.at[slot],
                    xcol(dx, 1 - e),
                )
    for k, e in enumerate((0, 2, 1)):
        swaps[k].wait_recv()
        for b in range(0, NT, PQ):
            rows = slice(b * KH, b * KH + qrows)
            pieces = []
            for n in range(b, b + PQ):
                both = jnp.concatenate([rfull[m, e, n * KH : (n + 1) * KH, :] for m in range(2)], axis=0)
                high = both.astype(bf16)
                low = (both - high.astype(f32)).astype(bf16)
                three = mm(stack, high)
                pieces.append(three[:KH] + three[KH : 2 * KH] + (three[2 * KH :] + mm(w1, low)))
            value = jnp.concatenate(pieces, axis=0)
            pr_send[e, rows, :] = value.astype(bf16)
            if e == 1:
                pacc[rows, :] = value
            owner = b // PQ
            dx = lax.rem(owner - x + X, X)
            slot = dx * 3 + e
            cp = remote(
                pr_send.at[e, pl.ds(b * KH, qrows)], pr_recv.at[slot], pr_s.at[slot], pr_r.at[slot],
                dev(owner, lax.rem(c + 2 * (owner - x) + 1 - e + 4 * C, C)),
            )
            if e == 1:
                pl.when(owner != x)(cp.start)
            else:
                cp.start()

    for n in range(2 * NT):
        three = mm(stack, row_pair(n))
        value = three[:KH] + three[KH : 2 * KH] + three[2 * KH :]
        bp[(NT + n) * KH : (NT + n + 1) * KH, :] = value.astype(bf16)
    for g in range(NT):
        first = (NT + 2 * g) * KH
        pieces = [
            bp[first + o * KH : first + (o + 1) * KH, s * B : (s + 1) * B] for o in range(2) for s in range(2)
        ]
        bpt[:, g * B : (g + 1) * B] = jnp.concatenate(pieces, axis=0).T

    quarter = pl.ds(pl.multiple_of(x * qrows, qrows), qrows)
    total = pacc[quarter, :]
    for slot, cp in pr_copies.items():
        cp.wait_recv()
        total = total + pr_recv[slot].astype(f32)
    pending += list(pr_copies.values())
    prb[1, quarter, :] = total.astype(bf16)
    copies = []
    for dx in sorted(range(X), key=lambda dx: -min(dx, X - dx)):
        for e in range(3):
            if dx == 0 and e == 1:
                continue
            slot = dx * 3 + e
            cp = remote(
                prb.at[1, quarter], prb.at[e, quarter], pa_s.at[slot], pa_r.at[slot], xcol(dx, e - 1)
            )
            cp.start()
            copies.append(cp)
    for cp in copies:
        cp.wait_recv()
    pending += copies

    def active(h, xx):
        return c - 2 * xx >= 0 if h == 0 else c - 2 * xx - 2 < 0

    nbr, nbc = 2 * nb * X, nb * C

    def lag_of(h, t):
        return h * nbc + c * nb + core * NT + t

    def pairs_of(lag, first, last):
        low = jnp.maximum(first, lag - (nbc - 1))
        return jnp.maximum(jnp.minimum(last, lag) - low + 1, 0).astype(f32)

    def measured(h, t):
        return wl[h, pl.ds(pl.multiple_of((core * NT + t + 1) * B, B), B), 0:B].astype(f32)

    order = sorted(range(1, X), key=lambda dx: -min(dx, X - dx)) + [0]
    tx_copies, xr_sends = [], []
    for h in range(2):
        across, sends = [], {}
        for k, dx in enumerate(order):
            across.append(
                remote(
                    tx_send.at[h, k], tx_recv.at[h, k], tx_s.at[h * X + k], tx_r.at[h * X + k],
                    dev(x, c, 1 - core),
                )
            )
            if dx > 0:
                sends[dx] = remote(
                    ch.at[h, k], xr.at[h, dx], xr_s.at[h * X + dx], xr_r.at[h * X + dx], dev(xat(dx), c)
                )
        tx_copies.append(across)
        xr_sends.append(sends)

        @pl.when(active(h, x))
        def _():
            for e in range(3):
                @pl.when(halves[e] == h)
                def _():
                    for i in range(NT):
                        n = e * NT + i
                        pair = prb[e, i * KH : (i + 1) * KH, :]
                        prx[n, 0:KH, :] = pair
                        prx[n, KH:, :B] = pair[:, B:]
                        if n > 0:
                            prx[n - 1, KH:, B:] = pair[:, :B]

                @pl.when(halves[e] != h)
                def _():
                    for i in range(NT):
                        n = e * NT + i
                        prx[n, 0:KH, :] = jnp.zeros((KH, 2 * B), bf16)
                        prx[n, KH:, :B] = jnp.zeros((KH, B), bf16)
                        if n > 0:
                            prx[n - 1, KH:, B:] = jnp.zeros((KH, B), bf16)

            def lag_pair(tp):
                right = prx[pl.ds(NT - 1 - tp, 2 * NT)].reshape(4 * NT * KH, 2 * B)
                return mm(bpt[...], right)

            def combine(k):
                dx = order[k]
                across[k].wait_recv()
                for i in range(LQ):
                    t = xat(dx) * LQ + i
                    n = pairs_of(lag_of(h, t), 2 * nb * x, 2 * nb * (x + 1) - 1)
                    value = tot[h, k, i] + tx_recv[h, k, i].astype(f32) - (0.5 * n) * measured(h, t)
                    if dx > 0:
                        ch[h, k, i] = value.astype(bf16)
                    else:
                        tot[h, k, i] = value
                if dx > 0:
                    sends[dx].start()

            for k, dx in enumerate(order):
                first = xat(dx) * (LQ // 2)
                for i in range(LQ // 2):
                    value = lag_pair((1 - core) * HB + first + i).astype(bf16)
                    tx_send[h, k, 2 * i] = value[:, B:]
                    tx_send[h, k, 2 * i + 1] = value[:, :B]
                across[k].start()
                for i in range(LQ // 2):
                    value = lag_pair(core * HB + first + i)
                    tot[h, k, 2 * i] = value[:, B:]
                    tot[h, k, 2 * i + 1] = value[:, :B]
                if k > 0:
                    combine(k - 1)
            combine(X - 1)

    has = [None, c < 2 * X]
    ag_copies, fx_copies = [], []

    def piece(h, xx):
        return out_ref.at[h, pl.ds(core * NT + xx * LQ, LQ)]

    for h in range(2):
        ag_copies.append(
            [
                remote(piece(h, x), piece(h, x), ag_s.at[h * X + dx], ag_r.at[h * X + dx], dev(xat(dx), c))
                for dx in range(1, X)
            ]
        )
        fx_copies.append(
            [
                remote(
                    piece(h, lax.rem(x - dx + X, X)), piece(h, lax.rem(x - dx + X, X)),
                    fx_s.at[h * X + dx], fx_r.at[h * X + dx], dev(x, c, 1 - core),
                )
                for dx in range(X)
            ]
        )

    def spread(h):
        @pl.when(jnp.logical_not(active(h, x)))
        def _():
            tot[h, X - 1] = jnp.zeros((LQ, B, B), f32)

        for dx in range(1, X):
            @pl.when(active(h, lax.rem(x - dx + X, X)))
            def _():
                xr_sends[h][dx].wait_recv()
                tot[h, X - 1] += xr[h, dx].astype(f32)

        for i in range(LQ):
            t = x * LQ + i
            n = pairs_of(lag_of(h, t), 0, nbr - 1)
            value = tot[h, X - 1, i] * (1.0 / jnp.maximum(n, 1.0))
            value = value + jnp.where(n > 0, 0.0, 0.5) * measured(h, t)
            out_ref[h, core * NT + t] = value.astype(bf16)
        for cp in ag_copies[h]:
            cp.start()
        fx_copies[h][0].start()

    def gather(h):
        for dx in range(1, X):
            ag_copies[h][dx - 1].wait_recv()
            fx_copies[h][dx].start()

    def settle(h):
        for cp in fx_copies[h]:
            cp.wait_recv()
        for cp in ag_copies[h] + fx_copies[h]:
            cp.wait_send()

    for part in (spread, gather, settle):
        part(0)
        pl.when(has[1])(functools.partial(part, 1))

    @pl.when(jnp.logical_not(has[1]))
    def _():
        for t in range(nb):
            out_ref[1, t] = (0.5 * wl[1, (t + 1) * B : (t + 2) * B, 0:B].astype(f32)).astype(bf16)

    for h in range(2):
        @pl.when(active(h, x))
        def _():
            for cp in tx_copies[h] + list(xr_sends[h].values()):
                cp.wait_send()

    for e in range(3):
        @pl.when(jnp.logical_not(om_self[e]))
        def _():
            om_copies[e].wait_send()

    for cp in pending:
        cp.wait_send()


def local(X, C, SDT, markov, omega):
    halves, nb = markov.shape[:2]
    NT = nb // 2
    PO, PQ, LQ = nb // C, NT // X, NT // X
    vmem, dma = pltpu.VMEM, pltpu.SemaphoreType.DMA
    scratch = [
        vmem((2, (nb + 2) * B, 2 * B), bf16),
        vmem((NT * KH, 2 * B), bf16),
        vmem((3, (NT + 2 * PQ - 2) * KH, 2 * B), bf16),
        vmem((2 * NT * KH, 2 * B), f32),
        vmem((2 * NT * KH, 2 * B), SDT),
        vmem((C, PO * KH, 2 * B), SDT),
        vmem((KH, 4 * KH), f32),
        vmem((X, KH, 4 * KH), f32),
        vmem((2 * KH, 2 * KH), f32),
        vmem((4 * NT * KH, 2 * B), bf16),
        vmem((B, NT * B), bf16),
        vmem((NT * KH, 2 * B), f32),
        vmem((3, NT * KH, 2 * B), bf16),
        vmem((3 * X, PQ * KH, 2 * B), bf16),
        vmem((3, NT * KH, 2 * B), bf16),
        vmem((3 * NT, 2 * KH, 2 * B), bf16),
        vmem((2, X, LQ, B, B), f32),
        vmem((2, X, LQ, B, B), bf16),
        vmem((2, X, LQ, B, B), bf16),
        vmem((2, X, LQ, B, B), bf16),
        vmem((2, X, LQ, B, B), bf16),
        vmem((2, 2 * NT * KH, 2 * B), bf16),
        vmem((KH, nb * B), bf16),
        vmem((4 * NT * KH, 2 * B), bf16),
        vmem((2, 3, NT * KH, 2 * B), f32),
        dma((3,)), dma((3,)),
        dma((4,)), dma,
        dma((3,)), dma((3,)), dma((C,)), dma((C,)), dma((C,)), dma((C,)),
        dma((X,)), dma((X,)), dma((C,)), dma((C,)),
        dma((3 * X,)), dma((3 * X,)), dma((3 * X,)), dma((3 * X,)),
        *[dma((2 * X,))] * 8,
    ]
    excess = pl.pallas_call(
        functools.partial(kernel, X, C, nb, SDT),
        out_shape=pltpu.VMEM((halves, nb, B, B), bf16),
        in_specs=[pl.BlockSpec(memory_space=pltpu.HBM)] * 2,
        out_specs=pl.BlockSpec(memory_space=pltpu.VMEM),
        scratch_shapes=scratch,
        compiler_params=pltpu.CompilerParams(
            collective_id=0, has_side_effects=True, vmem_limit_bytes=57 * 2**20
        ),
        name="cadzow",
    )(markov.reshape(halves, nb * B, B), omega.T)
    return 0.75 * markov.astype(f32) + 0.5 * excess.astype(f32)


def solution(mesh):
    X, C = mesh.shape["row"] // 2, mesh.shape["col"]
    in_specs = (P(None, "col", None, None), P("col", None))
    return jax.shard_map(
        functools.partial(local, X, C, bf16),
        mesh=mesh,
        in_specs=in_specs,
        out_specs=P(None, "col", None, None),
        check_vma=False,
    )
```

```python
import functools

import jax
import jax.numpy as jnp
from jax import lax
from jax.experimental import pallas as pl
from jax.experimental.pallas import tpu as pltpu
from jax.sharding import PartitionSpec as P

NS_STEPS = 8
norm_floor = 1e-06
highest = lax.Precision.HIGHEST
MESH = pl.DeviceIdType.MESH
KH = 32
B = 128
f32, bf16 = jnp.float32, jnp.bfloat16
NT_DIMS = (((1,), (1,)), ((), ()))


def mm(left, right, **kw):
    return jnp.dot(left, right, preferred_element_type=f32, **kw)


def mm_nt(left, right, **kw):
    return lax.dot_general(left, right, NT_DIMS, preferred_element_type=f32, **kw)


def kernel(
    X, C, nb, SDT,
    l_ref, om_ref, out_ref,
    wl, q, omp, acc, s_send, s_recv, g_own, gx_recv, p_ref,
    bp, bpt, pacc, pr_send, pr_recv, prb, prx, tot, tx_send, tx_recv, ch, xr,
    sg, om, sp, rfull, rf_s, rf_r, l_sem, om_sem, om_s, om_r, s_s, s_r, sw_s, sw_r, gx_s, gx_r, b_s, b_r,
    pr_s, pr_r, pa_s, pa_r, tx_s, tx_r, xr_s, xr_r, ag_s, ag_r, fx_s, fx_r,
):
    NT = nb // 2
    HB = NT // 2
    PO = nb // C
    PQ = NT // X
    LQ = NT // X
    r = lax.axis_index("row")
    c = lax.axis_index("col")
    x, core = r // 2, r % 2

    def dev(xx, cc, kk=None):
        return (xx * 2 + (core if kk is None else kk), cc)

    def col(dc):
        return lax.rem(c + dc + 4 * C, C)

    def xat(dx):
        return lax.rem(x + dx, X)

    def xcol(dx, delta):
        xx = xat(dx)
        return dev(xx, lax.rem(c + 2 * (xx - x) + delta + 4 * C, C))

    def remote(src, dst, send, recv, device):
        return pltpu.make_async_remote_copy(
            src_ref=src, dst_ref=dst, send_sem=send, recv_sem=recv, device_id=device, device_id_type=MESH
        )

    halves = [jnp.where(c - 2 * x - e < 0, 1, 0).astype(jnp.int32) for e in range(3)]

    barrier = pltpu.get_barrier_semaphore()
    peers = [dev(x, col(dc)) for dc in range(1, C)]
    for dx in range(1, X):
        peers += [xcol(dx, delta) for delta in (-1, 0, 1)] + [dev(xat(dx), c)]
    peers.append(dev(x, c, 1 - core))
    for peer in peers:
        pl.semaphore_signal(barrier, inc=1, device_id=peer, device_id_type=MESH)

    loads = []
    for h in range(2):
        for s in range(2):
            loads.append(
                pltpu.make_async_copy(
                    l_ref.at[h],
                    wl.at[h, pl.ds((1 + s) * B, nb * B), pl.ds(s * B, B)],
                    l_sem.at[2 * h + s],
                )
            )
    for cp in loads:
        cp.start()
    half_rank = pl.ds(pl.multiple_of(core * KH, KH), KH)
    om_load = pltpu.make_async_copy(om_ref.at[half_rank], om, om_sem)
    om_load.start()
    zero = jnp.zeros((B, B), bf16)
    for h in range(2):
        wl[h, 0:B, 0:B] = zero
        wl[h, 0:B, B:] = zero
        wl[h, B : 2 * B, B:] = zero
        wl[h, (nb + 1) * B :, 0:B] = zero
    sp[0 : NT * KH, :] = jnp.zeros((NT * KH, 2 * B), bf16)
    sp[3 * NT * KH :, :] = jnp.zeros((NT * KH, 2 * B), bf16)
    PAD = PQ - 1
    for e in range(3):
        omp[e, 0 : PAD * KH, :] = jnp.zeros((PAD * KH, 2 * B), bf16)
        omp[e, (PAD + NT) * KH :, :] = jnp.zeros((PAD * KH, 2 * B), bf16)
    om_load.wait()
    for w in range(NT):
        n = NT - 1 - w
        q[n * KH : (n + 1) * KH, :B] = om[:, (2 * w + 1) * B : (2 * w + 2) * B]
        q[n * KH : (n + 1) * KH, B:] = om[:, 2 * w * B : (2 * w + 1) * B]
    pl.semaphore_wait(barrier, len(peers))

    pending = []

    om_self = [lax.rem(2 * x + e, C) == 0 for e in range(3)]
    om_copies = []
    for e in range(3):
        cp = remote(q, omp.at[e, pl.ds(PAD * KH, NT * KH)], om_s.at[e], om_r.at[e], dev(x, col(2 * x + e)))
        om_copies.append(cp)

        @pl.when(jnp.logical_not(om_self[e]))
        def _():
            cp.start()

        @pl.when(om_self[e])
        def _():
            omp[e, PAD * KH : (PAD + NT) * KH, :] = q[...]

    for cp in loads:
        cp.wait()

    def lags(e, tau):
        return wl[halves[e], tau * 2 * B : (tau + 1) * 2 * B, :]

    srows, brows = PO * KH, PQ * KH
    s_copies = []

    def send_sketch(first, last):
        for i in range(last - first):
            dst = first + lax.rem(c + i, last - first)
            dc = lax.rem(dst - c + C, C)
            cp = remote(
                s_send.at[pl.ds(pl.multiple_of(dst * srows, srows), srows)], s_recv.at[dc], s_s.at[dc], s_r.at[dc], dev(x, dst)
            )
            pl.when(dst != c)(cp.start)

    started = set()
    for e in range(3):
        @pl.when(jnp.logical_not(om_self[e]))
        def _():
            om_copies[e].wait_recv()

        for b in range(0, 2 * NT, PQ):
            value = None
            for tau in range(NT + 1):
                n = b + NT - tau - e * NT
                if -PQ < n < NT:
                    left = omp[e, (PAD + n) * KH : (PAD + n) * KH + brows, :]
                    term = mm_nt(left, lags(e, tau))
                    value = term if value is None else value + term
            if value is None:
                continue
            rows = slice(b * KH, b * KH + brows)
            if b in started:
                value = value + acc[rows, :]
            started.add(b)
            acc[rows, :] = value
            if (e == 1 and b < NT) or e == 2:
                s_send[rows, :] = value.astype(SDT)
        if e > 0:
            send_sketch((e - 1) * C // 2, e * C // 2)

    for dc in range(1, C):
        s_copies.append(
            remote(s_send.at[pl.ds(0, srows)], s_recv.at[dc], s_s.at[dc], s_r.at[dc], dev(x, col(dc)))
        )
    total = acc[pl.ds(pl.multiple_of(c * srows, srows), srows), :]
    for dc in range(1, C):
        s_copies[dc - 1].wait_recv()
        total = total + s_recv[dc].astype(f32)
    pending += s_copies
    mine = pl.ds(pl.multiple_of(c * srows, srows), srows)
    sg[core, mine, :] = total.astype(bf16)
    b_copies = {}
    side = 4 if C % 4 == 0 else 1

    def hops(dc):
        y, z = dc % side, dc // side
        return min(y, side - y) + min(z, C // side - z)

    for dc in sorted(range(1, C), key=lambda dc: -hops(dc)):
        b_copies[dc] = remote(sg.at[core, mine], sg.at[core, mine], b_s.at[dc], b_r.at[dc], dev(x, col(dc)))
        b_copies[dc].start()

    def row_pair(n):
        return jnp.concatenate(
            [sg[k, pl.ds(pl.multiple_of(n * KH, KH), KH), :] for k in range(2)], axis=0
        )

    groups = C // side
    group = [lax.rem(c // side + g, groups) for g in range(groups)]
    grows = side * srows
    overs = []
    for g in range(groups):
        for y in range(side):
            dc = lax.rem(c - (group[g] * side + y) + C, C)
            cp = remote(sg.at[core, mine], sg.at[core, mine], b_s.at[dc], b_r.at[dc], dev(x, c, 1 - core))
            pl.when(dc != 0)(cp.wait_recv)
        at = sg.at[core, pl.ds(pl.multiple_of(group[g] * grows, grows), grows)]
        overs.append(remote(at, at, sw_s.at[g], sw_r.at[g], dev(x, c, 1 - core)))
        overs[g].start()
    gram = None
    for g in range(groups):
        overs[g].wait_recv()
        for i in range(side * PO):
            both = row_pair(group[g] * (side * PO) + i)
            term = mm_nt(both, both)
            gram = term if gram is None else gram + term
    g_own[...] = jnp.concatenate([gram[:KH], gram[KH:]], axis=1)
    gx_copies = []
    for dx in range(1, X):
        cp = remote(g_own, gx_recv.at[dx], gx_s.at[dx], gx_r.at[dx], dev(xat(dx), c))
        cp.start()
        gx_copies.append(cp)
    sp[NT * KH : 3 * NT * KH, :] = sg[core]
    qrows = PQ * KH
    swaps = []
    for e in (0, 2, 1):
        for b in range(0, NT, PQ):
            value = None
            for tau in range(NT + 1):
                if (e == 0 and b + PQ - 1 < NT - tau) or (e == 2 and b >= NT - tau):
                    continue
                first = (e * NT + b + tau) * KH
                term = mm(sp[first : first + qrows, :], lags(e, tau))
                value = term if value is None else value + term
            rfull[core, e, b * KH : b * KH + qrows, :] = value
        at = rfull.at[core, e]
        cp = remote(at, at, rf_s.at[e], rf_r.at[e], dev(x, c, 1 - core))
        cp.start()
        swaps.append(cp)

    packed = g_own[...]
    for dx in range(1, X):
        gx_copies[dx - 1].wait_recv()
        packed = packed + gx_recv[dx]
    pending += [*b_copies.values(), *overs, *gx_copies, *swaps]
    gram = jnp.concatenate([packed[:, : 2 * KH], packed[:, 2 * KH :]], axis=0)

    eye = (
        lax.broadcasted_iota(jnp.int32, (2 * KH, 2 * KH), 0)
        == lax.broadcasted_iota(jnp.int32, (2 * KH, 2 * KH), 1)
    ).astype(f32)
    trace = jnp.sum(gram * eye)
    scale = 1.0 / jnp.sqrt(jnp.full((1, 1), trace, f32) + norm_floor)
    inner = gram * (scale * scale)
    prod = None
    for sweep in range(NS_STEPS):
        a = 1.5 * eye - 0.5 * inner
        prod = a if prod is None else mm(prod, a, precision=highest)
        if sweep < NS_STEPS - 1:
            inner = mm(a, mm(inner, a, precision=highest), precision=highest)
    p_ref[...] = prod * scale
    weights = p_ref[half_rank, :]
    w1 = weights.astype(bf16)
    rest = weights - w1.astype(f32)
    w2 = rest.astype(bf16)
    w3 = (rest - w2.astype(f32)).astype(bf16)
    stack = jnp.concatenate([w1, w2, w3], axis=0)

    pr_copies = {}
    quarter = pl.ds(pl.multiple_of(x * qrows, qrows), qrows)
    for k, e in enumerate((0, 2, 1)):
        swaps[k].wait_recv()
        for dx in sorted(range(X), key=lambda dx: -min(dx, X - dx)):
            first = xat(dx) * qrows
            rows = pl.ds(pl.multiple_of(first, qrows), qrows)
            pieces = []
            for n in range(PQ):
                at = pl.ds(pl.multiple_of(first + n * KH, KH), KH)
                both = jnp.concatenate([rfull[m, e, at, :] for m in range(2)], axis=0)
                high = both.astype(bf16)
                low = (both - high.astype(f32)).astype(bf16)
                three = mm(stack, high)
                pieces.append(three[:KH] + three[KH : 2 * KH] + (three[2 * KH :] + mm(w1, low)))
            value = jnp.concatenate(pieces, axis=0)
            if dx == 0 and e == 1:
                pacc[...] = value
                continue
            pr_send[e, rows, :] = value.astype(bf16)
            slot = dx * 3 + e
            cp = remote(
                pr_send.at[e, rows], pr_recv.at[slot], pr_s.at[slot], pr_r.at[slot], xcol(dx, 1 - e)
            )
            cp.start()
            pr_copies[slot] = cp

    for n in range(2 * NT):
        three = mm(stack, row_pair(n))
        value = three[:KH] + three[KH : 2 * KH] + three[2 * KH :]
        bp[(NT + n) * KH : (NT + n + 1) * KH, :] = value.astype(bf16)
    for g in range(NT):
        first = (NT + 2 * g) * KH
        pieces = [
            bp[first + o * KH : first + (o + 1) * KH, s * B : (s + 1) * B] for o in range(2) for s in range(2)
        ]
        bpt[:, g * B : (g + 1) * B] = jnp.concatenate(pieces, axis=0).T

    total = pacc[...]
    for slot, cp in pr_copies.items():
        cp.wait_recv()
        total = total + pr_recv[slot].astype(f32)
    pending += list(pr_copies.values())
    prb[1, quarter, :] = total.astype(bf16)
    copies = []
    for dx in sorted(range(X), key=lambda dx: -min(dx, X - dx)):
        for e in range(3):
            if dx == 0 and e == 1:
                continue
            slot = dx * 3 + e
            cp = remote(
                prb.at[1, quarter], prb.at[e, quarter], pa_s.at[slot], pa_r.at[slot], xcol(dx, e - 1)
            )
            cp.start()
            copies.append(cp)
    for cp in copies:
        cp.wait_recv()
    pending += copies

    def active(h, xx):
        return c - 2 * xx >= 0 if h == 0 else c - 2 * xx - 2 < 0

    nbr, nbc = 2 * nb * X, nb * C

    def lag_of(h, t):
        return h * nbc + c * nb + core * NT + t

    def pairs_of(lag, first, last):
        low = jnp.maximum(first, lag - (nbc - 1))
        return jnp.maximum(jnp.minimum(last, lag) - low + 1, 0).astype(f32)

    def measured(h, t):
        return wl[h, pl.ds(pl.multiple_of((core * NT + t + 1) * B, B), B), 0:B].astype(f32)

    order = sorted(range(1, X), key=lambda dx: -min(dx, X - dx)) + [0]
    tx_copies, xr_sends = [], []
    for h in range(2):
        across, sends = [], {}
        for k, dx in enumerate(order):
            across.append(
                remote(
                    tx_send.at[h, k], tx_recv.at[h, k], tx_s.at[h * X + k], tx_r.at[h * X + k],
                    dev(x, c, 1 - core),
                )
            )
            if dx > 0:
                sends[dx] = remote(
                    ch.at[h, k], xr.at[h, dx], xr_s.at[h * X + dx], xr_r.at[h * X + dx], dev(xat(dx), c)
                )
        tx_copies.append(across)
        xr_sends.append(sends)

        @pl.when(active(h, x))
        def _():
            for e in range(3):
                @pl.when(halves[e] == h)
                def _():
                    for i in range(NT):
                        n = e * NT + i
                        pair = prb[e, i * KH : (i + 1) * KH, :]
                        prx[n, 0:KH, :] = pair
                        prx[n, KH:, :B] = pair[:, B:]
                        if n > 0:
                            prx[n - 1, KH:, B:] = pair[:, :B]

                @pl.when(halves[e] != h)
                def _():
                    for i in range(NT):
                        n = e * NT + i
                        prx[n, 0:KH, :] = jnp.zeros((KH, 2 * B), bf16)
                        prx[n, KH:, :B] = jnp.zeros((KH, B), bf16)
                        if n > 0:
                            prx[n - 1, KH:, B:] = jnp.zeros((KH, B), bf16)

            def lag_pair(tp):
                right = prx[pl.ds(NT - 1 - tp, 2 * NT)].reshape(4 * NT * KH, 2 * B)
                return mm(bpt[...], right)

            def combine(k):
                dx = order[k]
                across[k].wait_recv()
                for i in range(LQ):
                    t = xat(dx) * LQ + i
                    n = pairs_of(lag_of(h, t), 2 * nb * x, 2 * nb * (x + 1) - 1)
                    value = tot[h, k, i] + tx_recv[h, k, i].astype(f32) - (0.5 * n) * measured(h, t)
                    if dx > 0:
                        ch[h, k, i] = value.astype(bf16)
                    else:
                        tot[h, k, i] = value
                if dx > 0:
                    sends[dx].start()

            for k, dx in enumerate(order):
                first = xat(dx) * (LQ // 2)
                for i in range(LQ // 2):
                    value = lag_pair((1 - core) * HB + first + i).astype(bf16)
                    tx_send[h, k, 2 * i] = value[:, B:]
                    tx_send[h, k, 2 * i + 1] = value[:, :B]
                across[k].start()
                for i in range(LQ // 2):
                    value = lag_pair(core * HB + first + i)
                    tot[h, k, 2 * i] = value[:, B:]
                    tot[h, k, 2 * i + 1] = value[:, :B]
                if k > 0:
                    combine(k - 1)
            combine(X - 1)

    has = [None, c < 2 * X]
    ag_copies, fx_copies = [], []

    def piece(h, xx):
        return out_ref.at[h, pl.ds(core * NT + xx * LQ, LQ)]

    for h in range(2):
        ag_copies.append(
            [
                remote(piece(h, x), piece(h, x), ag_s.at[h * X + dx], ag_r.at[h * X + dx], dev(xat(dx), c))
                for dx in range(1, X)
            ]
        )
        fx_copies.append(
            [
                remote(
                    piece(h, lax.rem(x - dx + X, X)), piece(h, lax.rem(x - dx + X, X)),
                    fx_s.at[h * X + dx], fx_r.at[h * X + dx], dev(x, c, 1 - core),
                )
                for dx in range(X)
            ]
        )

    def spread(h):
        @pl.when(jnp.logical_not(active(h, x)))
        def _():
            tot[h, X - 1] = jnp.zeros((LQ, B, B), f32)

        for dx in range(1, X):
            @pl.when(active(h, lax.rem(x - dx + X, X)))
            def _():
                xr_sends[h][dx].wait_recv()
                tot[h, X - 1] += xr[h, dx].astype(f32)

        for i in range(LQ):
            t = x * LQ + i
            n = pairs_of(lag_of(h, t), 0, nbr - 1)
            value = tot[h, X - 1, i] * (1.0 / jnp.maximum(n, 1.0))
            value = value + jnp.where(n > 0, 0.0, 0.5) * measured(h, t)
            out_ref[h, core * NT + t] = value.astype(bf16)
        for cp in ag_copies[h]:
            cp.start()
        fx_copies[h][0].start()

    def gather(h):
        for dx in range(1, X):
            ag_copies[h][dx - 1].wait_recv()
            fx_copies[h][dx].start()

    def settle(h):
        for cp in fx_copies[h]:
            cp.wait_recv()
        for cp in ag_copies[h] + fx_copies[h]:
            cp.wait_send()

    for part in (spread, gather, settle):
        part(0)
        pl.when(has[1])(functools.partial(part, 1))

    @pl.when(jnp.logical_not(has[1]))
    def _():
        for t in range(nb):
            out_ref[1, t] = (0.5 * wl[1, (t + 1) * B : (t + 2) * B, 0:B].astype(f32)).astype(bf16)

    for h in range(2):
        @pl.when(active(h, x))
        def _():
            for cp in tx_copies[h] + list(xr_sends[h].values()):
                cp.wait_send()

    for e in range(3):
        @pl.when(jnp.logical_not(om_self[e]))
        def _():
            om_copies[e].wait_send()

    for cp in pending:
        cp.wait_send()


def local(X, C, SDT, markov, omega):
    halves, nb = markov.shape[:2]
    NT = nb // 2
    PO, PQ, LQ = nb // C, NT // X, NT // X
    vmem, dma = pltpu.VMEM, pltpu.SemaphoreType.DMA
    scratch = [
        vmem((2, (nb + 2) * B, 2 * B), bf16),
        vmem((NT * KH, 2 * B), bf16),
        vmem((3, (NT + 2 * PQ - 2) * KH, 2 * B), bf16),
        vmem((2 * NT * KH, 2 * B), f32),
        vmem((2 * NT * KH, 2 * B), SDT),
        vmem((C, PO * KH, 2 * B), SDT),
        vmem((KH, 4 * KH), f32),
        vmem((X, KH, 4 * KH), f32),
        vmem((2 * KH, 2 * KH), f32),
        vmem((4 * NT * KH, 2 * B), bf16),
        vmem((B, NT * B), bf16),
        vmem((PQ * KH, 2 * B), f32),
        vmem((3, NT * KH, 2 * B), bf16),
        vmem((3 * X, PQ * KH, 2 * B), bf16),
        vmem((3, NT * KH, 2 * B), bf16),
        vmem((3 * NT, 2 * KH, 2 * B), bf16),
        vmem((2, X, LQ, B, B), f32),
        vmem((2, X, LQ, B, B), bf16),
        vmem((2, X, LQ, B, B), bf16),
        vmem((2, X, LQ, B, B), bf16),
        vmem((2, X, LQ, B, B), bf16),
        vmem((2, 2 * NT * KH, 2 * B), bf16),
        vmem((KH, nb * B), bf16),
        vmem((4 * NT * KH, 2 * B), bf16),
        vmem((2, 3, NT * KH, 2 * B), f32),
        dma((3,)), dma((3,)),
        dma((4,)), dma,
        dma((3,)), dma((3,)), dma((C,)), dma((C,)), dma((C,)), dma((C,)),
        dma((X,)), dma((X,)), dma((C,)), dma((C,)),
        dma((3 * X,)), dma((3 * X,)), dma((3 * X,)), dma((3 * X,)),
        *[dma((2 * X,))] * 8,
    ]
    excess = pl.pallas_call(
        functools.partial(kernel, X, C, nb, SDT),
        out_shape=pltpu.VMEM((halves, nb, B, B), bf16),
        in_specs=[pl.BlockSpec(memory_space=pltpu.HBM)] * 2,
        out_specs=pl.BlockSpec(memory_space=pltpu.VMEM),
        scratch_shapes=scratch,
        compiler_params=pltpu.CompilerParams(
            collective_id=0, has_side_effects=True, vmem_limit_bytes=57 * 2**20
        ),
        name="cadzow",
    )(markov.reshape(halves, nb * B, B), omega.T)
    return 0.75 * markov.astype(f32) + 0.5 * excess.astype(f32)


def solution(mesh):
    X, C = mesh.shape["row"] // 2, mesh.shape["col"]
    in_specs = (P(None, "col", None, None), P("col", None))
    return jax.shard_map(
        functools.partial(local, X, C, bf16),
        mesh=mesh,
        in_specs=in_specs,
        out_specs=P(None, "col", None, None),
        check_vma=False,
    )
```

```python
import functools

import jax
import jax.numpy as jnp
from jax import lax
from jax.experimental import pallas as pl
from jax.experimental.pallas import tpu as pltpu
from jax.sharding import PartitionSpec as P

NS_STEPS = 8
norm_floor = 1e-06
highest = lax.Precision.HIGHEST
MESH = pl.DeviceIdType.MESH
KH = 32
B = 128
f32, bf16 = jnp.float32, jnp.bfloat16
NT_DIMS = (((1,), (1,)), ((), ()))


def mm(left, right, **kw):
    return jnp.dot(left, right, preferred_element_type=f32, **kw)


def mm_nt(left, right, **kw):
    return lax.dot_general(left, right, NT_DIMS, preferred_element_type=f32, **kw)


def kernel(
    X, C, nb, SDT,
    l_ref, om_ref, out_ref,
    wl, q, omp, acc, s_send, s_recv, g_own, gx_recv, p_ref,
    bp, bpt, pacc, pr_send, pr_recv, prb, prx, tot, tx_send, tx_recv, ch, xr,
    sg, om, sp, rfull, rf_s, rf_r, l_sem, om_sem, om_s, om_r, s_s, s_r, sw_s, sw_r, gx_s, gx_r, b_s, b_r,
    pr_s, pr_r, pa_s, pa_r, tx_s, tx_r, xr_s, xr_r, ag_s, ag_r, fx_s, fx_r,
):
    NT = nb // 2
    HB = NT // 2
    PO = nb // C
    PQ = NT // X
    LQ = NT // X
    r = lax.axis_index("row")
    c = lax.axis_index("col")
    x, core = r // 2, r % 2

    def dev(xx, cc, kk=None):
        return (xx * 2 + (core if kk is None else kk), cc)

    def col(dc):
        return lax.rem(c + dc + 4 * C, C)

    def xat(dx):
        return lax.rem(x + dx, X)

    def xcol(dx, delta):
        xx = xat(dx)
        return dev(xx, lax.rem(c + 2 * (xx - x) + delta + 4 * C, C))

    def remote(src, dst, send, recv, device):
        return pltpu.make_async_remote_copy(
            src_ref=src, dst_ref=dst, send_sem=send, recv_sem=recv, device_id=device, device_id_type=MESH
        )

    halves = [jnp.where(c - 2 * x - e < 0, 1, 0).astype(jnp.int32) for e in range(3)]

    barrier = pltpu.get_barrier_semaphore()
    side = 4 if C % 4 == 0 else 1

    def hops(dc):
        y, z = dc % side, dc // side
        return min(y, side - y) + min(z, C // side - z)

    far_cols = sorted(range(1, C), key=lambda dc: -hops(dc))
    far_x = sorted(range(1, X), key=lambda dx: -min(dx, X - dx))
    peers = [xcol(dx, delta) for dx in far_x for delta in (-1, 0, 1)]
    peers += [dev(x, col(dc)) for dc in far_cols]
    peers += [dev(xat(dx), c) for dx in far_x] + [dev(x, c, 1 - core)]
    for peer in peers:
        pl.semaphore_signal(barrier, inc=1, device_id=peer, device_id_type=MESH)

    loads = []
    for h in range(2):
        for s in range(2):
            loads.append(
                pltpu.make_async_copy(
                    l_ref.at[h],
                    wl.at[h, pl.ds((1 + s) * B, nb * B), pl.ds(s * B, B)],
                    l_sem.at[2 * h + s],
                )
            )
    for cp in loads:
        cp.start()
    half_rank = pl.ds(pl.multiple_of(core * KH, KH), KH)
    om_load = pltpu.make_async_copy(om_ref.at[half_rank], om, om_sem)
    om_load.start()
    zero = jnp.zeros((B, B), bf16)
    for h in range(2):
        wl[h, 0:B, 0:B] = zero
        wl[h, 0:B, B:] = zero
        wl[h, B : 2 * B, B:] = zero
        wl[h, (nb + 1) * B :, 0:B] = zero
    sp[0 : NT * KH, :] = jnp.zeros((NT * KH, 2 * B), bf16)
    sp[3 * NT * KH :, :] = jnp.zeros((NT * KH, 2 * B), bf16)
    PAD = PQ - 1
    for e in range(3):
        omp[e, 0 : PAD * KH, :] = jnp.zeros((PAD * KH, 2 * B), bf16)
        omp[e, (PAD + NT) * KH :, :] = jnp.zeros((PAD * KH, 2 * B), bf16)
    om_load.wait()
    for w in range(NT):
        n = NT - 1 - w
        q[n * KH : (n + 1) * KH, :B] = om[:, (2 * w + 1) * B : (2 * w + 2) * B]
        q[n * KH : (n + 1) * KH, B:] = om[:, 2 * w * B : (2 * w + 1) * B]
    pl.semaphore_wait(barrier, len(peers))

    pending = []

    om_self = [lax.rem(2 * x + e, C) == 0 for e in range(3)]
    om_copies = []
    for e in range(3):
        cp = remote(q, omp.at[e, pl.ds(PAD * KH, NT * KH)], om_s.at[e], om_r.at[e], dev(x, col(2 * x + e)))
        om_copies.append(cp)

        @pl.when(jnp.logical_not(om_self[e]))
        def _():
            cp.start()

        @pl.when(om_self[e])
        def _():
            omp[e, PAD * KH : (PAD + NT) * KH, :] = q[...]

    for cp in loads:
        cp.wait()

    def lags(e, tau):
        return wl[halves[e], tau * 2 * B : (tau + 1) * 2 * B, :]

    srows, brows = PO * KH, PQ * KH
    s_copies = []

    def send_sketch(first, last):
        for dst in range(first, last):
            dc = lax.rem(dst - c + C, C)
            cp = remote(
                s_send.at[pl.ds(dst * srows, srows)], s_recv.at[dc], s_s.at[dc], s_r.at[dc], dev(x, dst)
            )
            pl.when(dst != c)(cp.start)

    started = set()
    for e in range(3):
        @pl.when(jnp.logical_not(om_self[e]))
        def _():
            om_copies[e].wait_recv()

        for b in range(0, 2 * NT, PQ):
            value = None
            for tau in range(NT + 1):
                n = b + NT - tau - e * NT
                if -PQ < n < NT:
                    left = omp[e, (PAD + n) * KH : (PAD + n) * KH + brows, :]
                    term = mm_nt(left, lags(e, tau))
                    value = term if value is None else value + term
            if value is None:
                continue
            rows = slice(b * KH, b * KH + brows)
            if b in started:
                value = value + acc[rows, :]
            started.add(b)
            acc[rows, :] = value
            if (e == 1 and b < NT) or e == 2:
                s_send[rows, :] = value.astype(SDT)
        if e > 0:
            send_sketch((e - 1) * C // 2, e * C // 2)

    for dc in range(1, C):
        s_copies.append(
            remote(s_send.at[pl.ds(0, srows)], s_recv.at[dc], s_s.at[dc], s_r.at[dc], dev(x, col(dc)))
        )
    total = acc[pl.ds(pl.multiple_of(c * srows, srows), srows), :]
    for dc in range(1, C):
        s_copies[dc - 1].wait_recv()
        total = total + s_recv[dc].astype(f32)
    pending += s_copies
    mine = pl.ds(pl.multiple_of(c * srows, srows), srows)
    sg[core, mine, :] = total.astype(bf16)
    b_copies = {}
    for dc in far_cols:
        b_copies[dc] = remote(sg.at[core, mine], sg.at[core, mine], b_s.at[dc], b_r.at[dc], dev(x, col(dc)))
        b_copies[dc].start()

    def row_pair(n):
        return jnp.concatenate(
            [sg[k, pl.ds(pl.multiple_of(n * KH, KH), KH), :] for k in range(2)], axis=0
        )

    groups = C // side
    group = [lax.rem(c // side + g, groups) for g in range(groups)]
    grows = side * srows
    overs = []
    for g in range(groups):
        for y in range(side):
            dc = lax.rem(c - (group[g] * side + y) + C, C)
            cp = remote(sg.at[core, mine], sg.at[core, mine], b_s.at[dc], b_r.at[dc], dev(x, c, 1 - core))
            pl.when(dc != 0)(cp.wait_recv)
        at = sg.at[core, pl.ds(pl.multiple_of(group[g] * grows, grows), grows)]
        overs.append(remote(at, at, sw_s.at[g], sw_r.at[g], dev(x, c, 1 - core)))
        overs[g].start()
    gram = None
    for g in range(groups):
        overs[g].wait_recv()
        for i in range(side * PO):
            both = row_pair(group[g] * (side * PO) + i)
            term = mm_nt(both, both)
            gram = term if gram is None else gram + term
    g_own[...] = jnp.concatenate([gram[:KH], gram[KH:]], axis=1)
    gx_copies = []
    for dx in range(1, X):
        cp = remote(g_own, gx_recv.at[dx], gx_s.at[dx], gx_r.at[dx], dev(xat(dx), c))
        cp.start()
        gx_copies.append(cp)
    sp[NT * KH : 3 * NT * KH, :] = sg[core]
    qrows = PQ * KH
    swaps = []
    for e in (0, 2, 1):
        for b in range(0, NT, PQ):
            value = None
            for tau in range(NT + 1):
                if (e == 0 and b + PQ - 1 < NT - tau) or (e == 2 and b >= NT - tau):
                    continue
                first = (e * NT + b + tau) * KH
                term = mm(sp[first : first + qrows, :], lags(e, tau))
                value = term if value is None else value + term
            rfull[core, e, b * KH : b * KH + qrows, :] = value
        at = rfull.at[core, e]
        cp = remote(at, at, rf_s.at[e], rf_r.at[e], dev(x, c, 1 - core))
        cp.start()
        swaps.append(cp)

    packed = g_own[...]
    for dx in range(1, X):
        gx_copies[dx - 1].wait_recv()
        packed = packed + gx_recv[dx]
    pending += [*b_copies.values(), *overs, *gx_copies, *swaps]
    gram = jnp.concatenate([packed[:, : 2 * KH], packed[:, 2 * KH :]], axis=0)

    eye = (
        lax.broadcasted_iota(jnp.int32, (2 * KH, 2 * KH), 0)
        == lax.broadcasted_iota(jnp.int32, (2 * KH, 2 * KH), 1)
    ).astype(f32)
    trace = jnp.sum(gram * eye)
    scale = 1.0 / jnp.sqrt(jnp.full((1, 1), trace, f32) + norm_floor)
    inner = gram * (scale * scale)
    prod = None
    for sweep in range(NS_STEPS):
        a = 1.5 * eye - 0.5 * inner
        prod = a if prod is None else mm(prod, a, precision=highest)
        if sweep < NS_STEPS - 1:
            inner = mm(a, mm(inner, a, precision=highest), precision=highest)
    p_ref[...] = prod * scale
    weights = p_ref[half_rank, :]
    w1 = weights.astype(bf16)
    rest = weights - w1.astype(f32)
    w2 = rest.astype(bf16)
    w3 = (rest - w2.astype(f32)).astype(bf16)
    stack = jnp.concatenate([w1, w2, w3], axis=0)

    pr_copies = {}
    for dx in range(X):
        for e in range(3):
            if dx > 0 or e != 1:
                slot = dx * 3 + e
                pr_copies[slot] = remote(
                    pr_send.at[e, pl.ds(0, qrows)], pr_recv.at[slot], pr_s.at[slot], pr_r.at[slot],
                    xcol(dx, 1 - e),
                )
    for k, e in enumerate((0, 2, 1)):
        swaps[k].wait_recv()
        for b in range(0, NT, PQ):
            rows = slice(b * KH, b * KH + qrows)
            pieces = []
            for n in range(b, b + PQ):
                both = jnp.concatenate([rfull[m, e, n * KH : (n + 1) * KH, :] for m in range(2)], axis=0)
                high = both.astype(bf16)
                low = (both - high.astype(f32)).astype(bf16)
                three = mm(stack, high)
                pieces.append(three[:KH] + three[KH : 2 * KH] + (three[2 * KH :] + mm(w1, low)))
            value = jnp.concatenate(pieces, axis=0)
            pr_send[e, rows, :] = value.astype(bf16)
            if e == 1:
                pacc[rows, :] = value
            owner = b // PQ
            dx = lax.rem(owner - x + X, X)
            slot = dx * 3 + e
            cp = remote(
                pr_send.at[e, pl.ds(b * KH, qrows)], pr_recv.at[slot], pr_s.at[slot], pr_r.at[slot],
                dev(owner, lax.rem(c + 2 * (owner - x) + 1 - e + 4 * C, C)),
            )
            if e == 1:
                pl.when(owner != x)(cp.start)
            else:
                cp.start()

    for n in range(2 * NT):
        three = mm(stack, row_pair(n))
        value = three[:KH] + three[KH : 2 * KH] + three[2 * KH :]
        bp[(NT + n) * KH : (NT + n + 1) * KH, :] = value.astype(bf16)
    for g in range(NT):
        first = (NT + 2 * g) * KH
        pieces = [
            bp[first + o * KH : first + (o + 1) * KH, s * B : (s + 1) * B] for o in range(2) for s in range(2)
        ]
        bpt[:, g * B : (g + 1) * B] = jnp.concatenate(pieces, axis=0).T

    quarter = pl.ds(pl.multiple_of(x * qrows, qrows), qrows)
    total = pacc[quarter, :]
    for slot, cp in pr_copies.items():
        cp.wait_recv()
        total = total + pr_recv[slot].astype(f32)
    pending += list(pr_copies.values())
    prb[1, quarter, :] = total.astype(bf16)
    copies = []
    for dx in sorted(range(X), key=lambda dx: -min(dx, X - dx)):
        for e in range(3):
            if dx == 0 and e == 1:
                continue
            slot = dx * 3 + e
            cp = remote(
                prb.at[1, quarter], prb.at[e, quarter], pa_s.at[slot], pa_r.at[slot], xcol(dx, e - 1)
            )
            cp.start()
            copies.append(cp)
    for cp in copies:
        cp.wait_recv()
    pending += copies

    def active(h, xx):
        return c - 2 * xx >= 0 if h == 0 else c - 2 * xx - 2 < 0

    nbr, nbc = 2 * nb * X, nb * C

    def lag_of(h, t):
        return h * nbc + c * nb + core * NT + t

    def pairs_of(lag, first, last):
        low = jnp.maximum(first, lag - (nbc - 1))
        return jnp.maximum(jnp.minimum(last, lag) - low + 1, 0).astype(f32)

    def measured(h, t):
        return wl[h, pl.ds(pl.multiple_of((core * NT + t + 1) * B, B), B), 0:B].astype(f32)

    order = sorted(range(1, X), key=lambda dx: -min(dx, X - dx)) + [0]
    tx_copies, xr_sends = [], []
    for h in range(2):
        across, sends = [], {}
        for k, dx in enumerate(order):
            across.append(
                remote(
                    tx_send.at[h, k], tx_recv.at[h, k], tx_s.at[h * X + k], tx_r.at[h * X + k],
                    dev(x, c, 1 - core),
                )
            )
            if dx > 0:
                sends[dx] = remote(
                    ch.at[h, k], xr.at[h, dx], xr_s.at[h * X + dx], xr_r.at[h * X + dx], dev(xat(dx), c)
                )
        tx_copies.append(across)
        xr_sends.append(sends)

        @pl.when(active(h, x))
        def _():
            for e in range(3):
                @pl.when(halves[e] == h)
                def _():
                    for i in range(NT):
                        n = e * NT + i
                        pair = prb[e, i * KH : (i + 1) * KH, :]
                        prx[n, 0:KH, :] = pair
                        prx[n, KH:, :B] = pair[:, B:]
                        if n > 0:
                            prx[n - 1, KH:, B:] = pair[:, :B]

                @pl.when(halves[e] != h)
                def _():
                    for i in range(NT):
                        n = e * NT + i
                        prx[n, 0:KH, :] = jnp.zeros((KH, 2 * B), bf16)
                        prx[n, KH:, :B] = jnp.zeros((KH, B), bf16)
                        if n > 0:
                            prx[n - 1, KH:, B:] = jnp.zeros((KH, B), bf16)

            def lag_pair(tp):
                right = prx[pl.ds(NT - 1 - tp, 2 * NT)].reshape(4 * NT * KH, 2 * B)
                return mm(bpt[...], right)

            def combine(k):
                dx = order[k]
                across[k].wait_recv()
                for i in range(LQ):
                    t = xat(dx) * LQ + i
                    n = pairs_of(lag_of(h, t), 2 * nb * x, 2 * nb * (x + 1) - 1)
                    value = tot[h, k, i] + tx_recv[h, k, i].astype(f32) - (0.5 * n) * measured(h, t)
                    if dx > 0:
                        ch[h, k, i] = value.astype(bf16)
                    else:
                        tot[h, k, i] = value
                if dx > 0:
                    sends[dx].start()

            for k, dx in enumerate(order):
                first = xat(dx) * (LQ // 2)
                for i in range(LQ // 2):
                    value = lag_pair((1 - core) * HB + first + i).astype(bf16)
                    tx_send[h, k, 2 * i] = value[:, B:]
                    tx_send[h, k, 2 * i + 1] = value[:, :B]
                across[k].start()
                for i in range(LQ // 2):
                    value = lag_pair(core * HB + first + i)
                    tot[h, k, 2 * i] = value[:, B:]
                    tot[h, k, 2 * i + 1] = value[:, :B]
                if k > 0:
                    combine(k - 1)
            combine(X - 1)

    has = [None, c < 2 * X]
    ag_copies, fx_copies = [], []

    def piece(h, xx):
        return out_ref.at[h, pl.ds(core * NT + xx * LQ, LQ)]

    for h in range(2):
        ag_copies.append(
            [
                remote(piece(h, x), piece(h, x), ag_s.at[h * X + dx], ag_r.at[h * X + dx], dev(xat(dx), c))
                for dx in range(1, X)
            ]
        )
        fx_copies.append(
            [
                remote(
                    piece(h, lax.rem(x - dx + X, X)), piece(h, lax.rem(x - dx + X, X)),
                    fx_s.at[h * X + dx], fx_r.at[h * X + dx], dev(x, c, 1 - core),
                )
                for dx in range(X)
            ]
        )

    def spread(h):
        @pl.when(jnp.logical_not(active(h, x)))
        def _():
            tot[h, X - 1] = jnp.zeros((LQ, B, B), f32)

        for dx in range(1, X):
            @pl.when(active(h, lax.rem(x - dx + X, X)))
            def _():
                xr_sends[h][dx].wait_recv()
                tot[h, X - 1] += xr[h, dx].astype(f32)

        for i in range(LQ):
            t = x * LQ + i
            n = pairs_of(lag_of(h, t), 0, nbr - 1)
            value = tot[h, X - 1, i] * (1.0 / jnp.maximum(n, 1.0))
            value = value + jnp.where(n > 0, 0.0, 0.5) * measured(h, t)
            out_ref[h, core * NT + t] = value.astype(bf16)
        for cp in ag_copies[h]:
            cp.start()
        fx_copies[h][0].start()

    def gather(h):
        for dx in range(1, X):
            ag_copies[h][dx - 1].wait_recv()
            fx_copies[h][dx].start()

    def settle(h):
        for cp in fx_copies[h]:
            cp.wait_recv()
        for cp in ag_copies[h] + fx_copies[h]:
            cp.wait_send()

    for part in (spread, gather, settle):
        part(0)
        pl.when(has[1])(functools.partial(part, 1))

    @pl.when(jnp.logical_not(has[1]))
    def _():
        for t in range(nb):
            out_ref[1, t] = (0.5 * wl[1, (t + 1) * B : (t + 2) * B, 0:B].astype(f32)).astype(bf16)

    for h in range(2):
        @pl.when(active(h, x))
        def _():
            for cp in tx_copies[h] + list(xr_sends[h].values()):
                cp.wait_send()

    for e in range(3):
        @pl.when(jnp.logical_not(om_self[e]))
        def _():
            om_copies[e].wait_send()

    for cp in pending:
        cp.wait_send()


def local(X, C, SDT, markov, omega):
    halves, nb = markov.shape[:2]
    NT = nb // 2
    PO, PQ, LQ = nb // C, NT // X, NT // X
    vmem, dma = pltpu.VMEM, pltpu.SemaphoreType.DMA
    scratch = [
        vmem((2, (nb + 2) * B, 2 * B), bf16),
        vmem((NT * KH, 2 * B), bf16),
        vmem((3, (NT + 2 * PQ - 2) * KH, 2 * B), bf16),
        vmem((2 * NT * KH, 2 * B), f32),
        vmem((2 * NT * KH, 2 * B), SDT),
        vmem((C, PO * KH, 2 * B), SDT),
        vmem((KH, 4 * KH), f32),
        vmem((X, KH, 4 * KH), f32),
        vmem((2 * KH, 2 * KH), f32),
        vmem((4 * NT * KH, 2 * B), bf16),
        vmem((B, NT * B), bf16),
        vmem((NT * KH, 2 * B), f32),
        vmem((3, NT * KH, 2 * B), bf16),
        vmem((3 * X, PQ * KH, 2 * B), bf16),
        vmem((3, NT * KH, 2 * B), bf16),
        vmem((3 * NT, 2 * KH, 2 * B), bf16),
        vmem((2, X, LQ, B, B), f32),
        vmem((2, X, LQ, B, B), bf16),
        vmem((2, X, LQ, B, B), bf16),
        vmem((2, X, LQ, B, B), bf16),
        vmem((2, X, LQ, B, B), bf16),
        vmem((2, 2 * NT * KH, 2 * B), bf16),
        vmem((KH, nb * B), bf16),
        vmem((4 * NT * KH, 2 * B), bf16),
        vmem((2, 3, NT * KH, 2 * B), f32),
        dma((3,)), dma((3,)),
        dma((4,)), dma,
        dma((3,)), dma((3,)), dma((C,)), dma((C,)), dma((C,)), dma((C,)),
        dma((X,)), dma((X,)), dma((C,)), dma((C,)),
        dma((3 * X,)), dma((3 * X,)), dma((3 * X,)), dma((3 * X,)),
        *[dma((2 * X,))] * 8,
    ]
    excess = pl.pallas_call(
        functools.partial(kernel, X, C, nb, SDT),
        out_shape=pltpu.VMEM((halves, nb, B, B), bf16),
        in_specs=[pl.BlockSpec(memory_space=pltpu.HBM)] * 2,
        out_specs=pl.BlockSpec(memory_space=pltpu.VMEM),
        scratch_shapes=scratch,
        compiler_params=pltpu.CompilerParams(
            collective_id=0, has_side_effects=True, vmem_limit_bytes=57 * 2**20
        ),
        name="cadzow",
    )(markov.reshape(halves, nb * B, B), omega.T)
    return 0.75 * markov.astype(f32) + 0.5 * excess.astype(f32)


def solution(mesh):
    X, C = mesh.shape["row"] // 2, mesh.shape["col"]
    in_specs = (P(None, "col", None, None), P("col", None))
    return jax.shard_map(
        functools.partial(local, X, C, bf16),
        mesh=mesh,
        in_specs=in_specs,
        out_specs=P(None, "col", None, None),
        check_vma=False,
    )
```
